256 devices in a mesh: ctx: 64 (over y, z, core), fsdp: 4 (over x).
Axes of the slice: x: 4, y: 4, z: 8, core: 2. Of those that a mesh axis runs over, the one named last changes fastest.
Arguments:
- hidden_rows: bfloat16 [8192, 2048], P('ctx', 'fsdp'), may hold values from -18 to 18
- w_qkv: bfloat16 [2048, 3072], P(None, 'fsdp'), may hold values from -4 to 4
- doc_lengths: int32 [8], replicated, may hold values from 1 to 4096, 8192 in all
- owners: int32 [8192], replicated, may hold values from 0 to 63, as said below
- context_grad: bfloat16 [8192, 2048], P('ctx', 'fsdp'), may hold values from -6 to 6
Outputs:
- context: bfloat16 [8192, 2048], P('ctx', 'fsdp')
- input_grad: float32 [8192, 2048], P('ctx', 'fsdp')
- weight_grad: float32 [2048, 3072], P('ctx', 'fsdp')
The draws below stay inside these ranges and needn't reach their ends.
Inputs may be any that keep to these rules, and one draw needn't show every extreme that they name: `owners`: each index of ctx owns exactly 128 rows. Of the 128 rows of one index of ctx, at most 4 go to any one owner, and in every draw some index sends exactly 4 rows to one owner. `doc_lengths`: 8 documents fill the 8192 rows; the longest has exactly 4096 tokens.
All inputs are finite; a program needn't handle non-finite values.
Results may differ from the reference program's by a relative error of at most 0.02.
Values may be sent and summed in bfloat16 or wider, within the bound.
No kernel may reach another device: no remote copies, remote signals or barrier semaphores. Data moves between devices by JAX's collectives and lax.ppermute only.
A program may use at most 128 MiB of HBM per device.

```python
import math
import jax
import jax.numpy as jnp
import numpy as np
from jax import lax

D = 2048
HD = 128
GROUP = 4
DOCS = 8
TOK_DEV = 128
KV_HEADS = 4
Q_HEADS = 16
TOKENS = 8192
CAP = 4
DOC_MOST = 4096
N_CTX = 64


def draw_hidden_rows(key, part):
    key = jax.random.fold_in(key, 5)
    key_list = jax.random.split(key, 2)
    base_draw = jnp.clip(jax.random.normal(key_list[0], (TOKENS, D), jnp.float32), -6.0, 6.0)
    scales = jnp.exp(jax.random.uniform(key_list[1], (TOKENS, 1), jnp.float32, math.log(0.3), math.log(3.0)))
    result = base_draw * scales
    return result.astype(jnp.bfloat16)


def draw_w_qkv(key, part):
    key = jax.random.fold_in(key, 7)
    columns = KV_HEADS * (GROUP + 2) * HD
    base_draw = jnp.clip(jax.random.normal(key, (D, columns), jnp.float32), -6.0, 6.0) * D ** (-0.5)
    return base_draw.astype(jnp.bfloat16)


def draw_owners(key, part):
    key = jax.random.fold_in(key, 13)
    key_list = jax.random.split(key, 5)
    devices = TOKENS // TOK_DEV
    pair_count = TOK_DEV // CAP
    offsets = jax.random.permutation(key_list[0], devices)[:2 * pair_count]
    first_load = jax.random.randint(key_list[1], (pair_count,), 0, CAP + 1).at[0].set(CAP)
    counts = jnp.concatenate([first_load, CAP - first_load])
    bounds = jnp.cumsum(counts)
    slot_ids = jnp.arange(TOK_DEV, dtype=jnp.int32)
    slot_pair = jnp.sum((slot_ids[:, None] >= bounds[None, :]).astype(jnp.int32), axis=1)
    slot_offset = offsets[slot_pair]
    relabel_source = jax.random.permutation(key_list[2], devices)
    relabel_target = jax.random.permutation(key_list[3], devices)
    slot_owner = relabel_target[(relabel_source[:, None] + slot_offset[None, :]) % devices]
    orders = jax.vmap(lambda each_key: jax.random.permutation(each_key, TOK_DEV))(jax.random.split(key_list[4], devices))
    result = jnp.take_along_axis(slot_owner, orders, axis=1)
    return result.reshape(TOKENS).astype(jnp.int32)


def levels(stream_key, shape, pieces, least, top_value):
    gain = 1.0
    for position, parts in pieces:
        draws = jax.random.uniform(jax.random.fold_in(jax.random.fold_in(stream_key, 6), position), (parts,), jnp.float32, least / len(pieces), top_value / len(pieces))
        gain = gain * jnp.repeat(jnp.exp(draws), shape[position] // parts).reshape((-1,) + (1,) * (len(shape) - 1 - position))
    return gain


def length_profile(amount, total, limit, slope):
    loads = [(1 << 20) // math.isqrt(grade ** slope) + 1 for grade in range(2, amount + 1)]
    rest, holding = total - limit - (amount - 1), [1] * (amount - 1)
    while rest > 0:
        candidates = [i for i in range(amount - 1) if holding[i] < limit]
        mass, budget = sum([loads[i] for i in candidates]), rest
        for i in candidates:
            extra = min(limit - holding[i], max(1, budget * loads[i] // mass), rest)
            holding[i] = holding[i] + extra
            rest = rest - extra
    return np.array([limit] + holding)


def ragged_sizes(own_key, number_of, total, bound, skew):
    if number_of == 2:
        one = jax.random.randint(own_key, (), max(1, total - bound), min(bound, total - 1) + 1)
        return jnp.stack([one, total - one])
    sizes = jnp.asarray(length_profile(number_of, total, bound, skew), jnp.int32)
    pairs = (number_of - 1) // 2
    giver, sink = sizes[1:1 + 2 * pairs:2], sizes[2:2 + 2 * pairs:2]
    margin = jnp.minimum(giver - 1, bound - sink)
    moved = jax.random.randint(jax.random.fold_in(own_key, 1), (pairs,), 0, 1 << 20) % (margin + 1)
    sizes = sizes.at[1:1 + 2 * pairs:2].set(giver - moved).at[2:2 + 2 * pairs:2].set(sink + moved)
    return sizes[jax.random.permutation(jax.random.fold_in(own_key, 2), number_of)]


def scatter_about(own_key, dims, scale, most, shards=(), held_as=jnp.bfloat16):
    factor_of = levels(own_key, dims, shards, -0.22, 0.18) if shards else 1.0
    values = jax.random.normal(own_key, dims, jnp.float32) * scale * factor_of
    return jnp.minimum(jnp.maximum(values, -most), most).astype(held_as)


def setup_inputs(seed: int = 0) -> dict:
    splits = jax.random.split(jax.random.key(seed), 6)
    hidden_rows = draw_hidden_rows(jax.random.fold_in(splits[5], 71), 0)
    w_qkv = draw_w_qkv(jax.random.fold_in(splits[5], 71), 0)
    doc_lengths = ragged_sizes(splits[2], DOCS, TOKENS, DOC_MOST, 2).astype(jnp.int32)
    owners = draw_owners(jax.random.fold_in(splits[5], 71), 0)
    context_grad = scatter_about(splits[4], (TOKENS, Q_HEADS * HD), 1.0, 6.0, ((0, 64), (1, 4)))
    return {"hidden_rows": hidden_rows, "w_qkv": w_qkv, "doc_lengths": doc_lengths, "owners": owners, "context_grad": context_grad}


epsilon = 1e-05
rope_base = 500000.0

def narrow(tensor):
    return lax.optimization_barrier(tensor.astype(jnp.bfloat16)).astype(jnp.float32)

def doc_tables(doc_lengths):
    doc_ends = jnp.cumsum(doc_lengths).astype(jnp.int32)
    doc_starts = doc_ends - doc_lengths
    row_ids = jnp.arange(TOKENS, dtype=jnp.int32)
    inside = (row_ids[:, None] >= doc_starts[None, :]) & (row_ids[:, None] < doc_ends[None, :])
    doc_number = jnp.arange(DOCS, dtype=jnp.int32)
    doc_id = lax.optimization_barrier(jnp.sum(jnp.where(inside, doc_number[None, :], 0), axis=1)).astype(jnp.int32)
    start_of = lax.optimization_barrier(jnp.sum(jnp.where(inside, doc_starts[None, :], 0), axis=1)).astype(jnp.int32)
    return (doc_id, (row_ids - start_of).astype(jnp.int32))

def rope_tables(positions):
    frequency = rope_base ** (-(2.0 * jnp.arange(HD // 2, dtype=jnp.float32)) / HD)
    angles = positions.astype(jnp.float32)[:, None] * frequency[None, :]
    return (jnp.cos(angles)[:, None, :], jnp.sin(angles)[:, None, :])

def rotate(tensor, cosines, sines):
    half_width = tensor.shape[-1] // 2
    first_half = tensor[..., :half_width]
    second_half = tensor[..., half_width:]
    return jnp.concatenate([first_half * cosines - second_half * sines, second_half * cosines + first_half * sines], axis=-1)

def rotate_back(tensor, cosines, sines):
    half_width = tensor.shape[-1] // 2
    first_half = tensor[..., :half_width]
    second_half = tensor[..., half_width:]
    return jnp.concatenate([first_half * cosines + second_half * sines, second_half * cosines - first_half * sines], axis=-1)

def reference(hidden_rows, w_qkv, doc_lengths, owners, context_grad):
    score_scale = HD ** (-0.5)
    group_width = (GROUP + 2) * HD
    heads_width = GROUP * HD
    doc_id, doc_pos = doc_tables(doc_lengths)
    cosines, sines = rope_tables(doc_pos)
    onehot = (owners[:, None] == jnp.arange(N_CTX, dtype=jnp.int32)[None, :]).astype(jnp.int32)
    owner_rank = lax.optimization_barrier(jnp.sum((jnp.cumsum(onehot, axis=0) - onehot) * onehot, axis=1))
    owner_index = (owners * TOK_DEV + owner_rank).astype(jnp.int32)
    layout_rows = jnp.zeros((TOKENS,), jnp.int32).at[owner_index].set(jnp.arange(TOKENS, dtype=jnp.int32))
    rows_f32 = hidden_rows.astype(jnp.float32)
    inv_rms = lax.rsqrt(lax.optimization_barrier(jnp.mean(rows_f32 * rows_f32, axis=1, keepdims=True)) + epsilon)
    normed = (rows_f32 * inv_rms).astype(jnp.bfloat16)
    grad_home = context_grad[owner_index].astype(jnp.float32)
    block_rows = min(512, TOKENS)
    blocks = TOKENS // block_rows
    contexts = []
    weight_parts = []
    input_total = jnp.zeros((TOKENS, D), jnp.float32)
    for head_group in range(KV_HEADS):
        w_part = w_qkv[:, head_group * group_width:(head_group + 1) * group_width]
        projected = jnp.dot(normed, w_part, preferred_element_type=jnp.float32)
        queries = narrow(rotate(projected[:, :heads_width].reshape(TOKENS, GROUP, HD), cosines, sines))
        key_vectors = narrow(rotate(projected[:, heads_width:heads_width + HD].reshape(TOKENS, 1, HD), cosines, sines).reshape(TOKENS, HD))
        value_vectors = narrow(projected[:, heads_width + HD:])
        grad_out = grad_home[:, head_group * heads_width:(head_group + 1) * heads_width].reshape(TOKENS, GROUP, HD)

        def block_probs(block_index):
            start_row = block_index * block_rows
            query_block = lax.dynamic_slice_in_dim(queries, start_row, block_rows)
            scores = jnp.einsum('rgd,nd->rgn', query_block, key_vectors) * score_scale
            query_doc = lax.dynamic_slice_in_dim(doc_id, start_row, block_rows)
            query_pos = lax.dynamic_slice_in_dim(doc_pos, start_row, block_rows)
            allowed = ((query_doc[:, None] == doc_id[None, :]) & (doc_pos[None, :] <= query_pos[:, None]))[:, None, :]
            running_max = lax.optimization_barrier(jnp.max(jnp.where(allowed, scores, -1e+30), axis=2, keepdims=True))
            log_totals = running_max + jnp.log(lax.optimization_barrier(jnp.sum(jnp.where(allowed, jnp.exp(scores - running_max), 0.0), axis=2, keepdims=True)))
            probs = jnp.where(allowed, jnp.exp(scores - log_totals), 0.0)
            return (probs, query_block)

        def forward_block(block_index):
            probs, query_block = block_probs(block_index)
            block_out = jnp.einsum('rgn,nd->rgd', probs, value_vectors, precision=lax.Precision.HIGHEST)
            return block_out.astype(jnp.bfloat16)
        outputs = lax.map(forward_block, jnp.arange(blocks, dtype=jnp.int32))
        context_home = outputs.reshape(TOKENS, GROUP, HD).astype(jnp.float32)
        delta_terms = lax.optimization_barrier(jnp.sum(grad_out * context_home, axis=2))

        def backward_block(running, block_index):
            key_sum, value_sum = running
            probs, query_block = block_probs(block_index)
            start_row = block_index * block_rows
            grad_block = lax.dynamic_slice_in_dim(grad_out, start_row, block_rows)
            delta_block = lax.dynamic_slice_in_dim(delta_terms, start_row, block_rows)
            dprobs = jnp.einsum('rgd,nd->rgn', grad_block, value_vectors)
            dscores = narrow(probs * (dprobs - delta_block[:, :, None]))
            query_part = score_scale * jnp.einsum('rgn,nd->rgd', dscores, key_vectors)
            key_sum = key_sum + score_scale * jnp.einsum('rgn,rgd->nd', dscores, query_block)
            value_sum = value_sum + jnp.einsum('rgn,rgd->nd', narrow(probs), grad_block)
            return ((key_sum, value_sum), query_part)
        zeros_kv = jnp.zeros((TOKENS, HD), jnp.float32)
        (key_sum, value_sum), query_parts = lax.scan(backward_block, (zeros_kv, zeros_kv), jnp.arange(blocks, dtype=jnp.int32))
        query_grad = rotate_back(query_parts.reshape(TOKENS, GROUP, HD), cosines, sines).reshape(TOKENS, heads_width)
        key_grad = rotate_back(key_sum.reshape(TOKENS, 1, HD), cosines, sines).reshape(TOKENS, HD)
        row_grads = jnp.concatenate([query_grad, key_grad, value_sum], axis=1).astype(jnp.bfloat16)
        weight_parts.append(jnp.dot(normed.T, row_grads, preferred_element_type=jnp.float32))
        input_total = input_total + jnp.dot(row_grads, w_part.T, preferred_element_type=jnp.float32)
        contexts.append(context_home.reshape(TOKENS, heads_width).astype(jnp.bfloat16))
    context = jnp.concatenate(contexts, axis=1)[layout_rows]
    inner = lax.optimization_barrier(jnp.mean(input_total * rows_f32, axis=1, keepdims=True))
    input_grad = inv_rms * input_total - rows_f32 * inv_rms * inv_rms * inv_rms * inner
    return (context, input_grad, jnp.concatenate(weight_parts, axis=1))
```

```python
import functools

import jax
import jax.numpy as jnp
from jax import lax
from jax.experimental import pallas as pl
from jax.experimental.pallas import tpu as pltpu
from jax.sharding import PartitionSpec as P

HD = 128
GROUP = 4
TOK = 128
NY, NZ, NC = 4, 8, 2
N_CTX = NY * NZ * NC
NX = 4
CAP = 4
SLOTS = N_CTX * CAP
VISITS = 3
QW = GROUP * TOK
epsilon = 1e-05
rope_base = 500000.0
scale = HD ** (-0.5)
log2e = 1.4426950408889634
masked = -1e30

f32, bf16, i32 = jnp.float32, jnp.bfloat16, jnp.int32

NT = (((1,), (1,)), ((), ()))
NN = (((1,), (0,)), ((), ()))
TN = (((0,), (0,)), ((), ()))


def dot(a, b, dims=NN):
    return lax.dot_general(a, b, dims, preferred_element_type=f32)


def call(kernel, outs, in_kinds, args, scratch=(), flops=10**8, moved=2 * 10**6, name=None):
    vm = pl.BlockSpec(memory_space=pltpu.VMEM)
    sm = pl.BlockSpec(memory_space=pltpu.SMEM)
    return pl.pallas_call(
        kernel,
        out_shape=[jax.ShapeDtypeStruct(s, d) for s, d in outs],
        in_specs=[sm if k == "s" else vm for k in in_kinds],
        out_specs=[vm] * len(outs),
        scratch_shapes=list(scratch),
        compiler_params=pltpu.CompilerParams(vmem_limit_bytes=48 * 1024 * 1024),
        cost_estimate=pl.CostEstimate(flops=flops, bytes_accessed=moved, transcendentals=0),
        name=name,
    )(*args)


def route_kernel(sc, owners, cg, mo_ref, mh_ref, send_ref):
    me = sc[0]
    mine = (owners[...] == me).astype(f32).astype(bf16)
    count = dot(mine, jnp.ones((TOK, TOK), bf16)).astype(bf16)
    slot_src = lax.broadcasted_iota(i32, (SLOTS, N_CTX), 0) // CAP
    source = lax.broadcasted_iota(i32, (SLOTS, N_CTX), 1)
    base = dot((source < slot_src).astype(f32).astype(bf16), count)
    here = dot((source == slot_src).astype(f32).astype(bf16), count)
    slot = lax.broadcasted_iota(i32, (SLOTS, TOK), 0)
    place = lax.broadcasted_iota(i32, (SLOTS, TOK), 1)
    rank = (slot % CAP).astype(f32)
    mo = jnp.where((base + rank == place.astype(f32)) & (rank < here), 1.0, 0.0).astype(bf16)
    mo_ref[...] = mo
    send_ref[...] = dot(mo, cg[...]).astype(bf16)
    own = jnp.broadcast_to(owners[pl.ds(me, 1), :].astype(f32), (TOK, TOK))
    earlier = lax.broadcasted_iota(i32, (TOK, TOK), 0) < lax.broadcasted_iota(i32, (TOK, TOK), 1)
    same = jnp.where((own == own.T) & earlier, 1.0, 0.0)
    home_slot = own[0:1, :] * CAP + jnp.sum(same, axis=0, keepdims=True)
    mh_ref[...] = jnp.where(slot.astype(f32) == home_slot, 1.0, 0.0).astype(bf16)


def grad_home_kernel(mh, arrived, out_ref):
    rows = dot(mh[...], arrived[...], TN).astype(bf16)
    for h in range(GROUP):
        out_ref[h * TOK : (h + 1) * TOK, :] = rows[:, h * HD : (h + 1) * HD]


def place_kernel(mo, arrived, out_ref):
    out_ref[...] = dot(mo[...], arrived[...], TN).astype(bf16)


def turn(t, c, s):
    return t * c + pltpu.roll(t, HD // 2, 1) * s


def turn_back(t, c, s):
    return t * c - pltpu.roll(t, HD // 2, 1) * s


def project_kernel(sc, h0, h1, h2, h3, w, cos, sin, q_ref, kv_ref, n0, n1, n2, n3, inv_ref, held):
    y, x = sc[1], sc[4]
    blocks = [h[...].astype(f32) for h in (h0, h1, h2, h3)]
    square = sum(jnp.sum(b * b, axis=1, keepdims=True) for b in blocks)
    inv = lax.rsqrt(square * (1.0 / (NX * 512)) + epsilon)
    inv_ref[...] = jnp.broadcast_to(inv, (TOK, HD))
    total = jnp.zeros((TOK, 768), f32)
    for s in range(NX):
        chunk = (x + NX - s) % NX
        normed = (blocks[s] * inv).astype(bf16)
        held[chunk] = normed
        total = total + dot(normed, w[pl.ds(pl.multiple_of(chunk * 512, 512), 512), :])
    for t, out in enumerate((n0, n1, n2, n3)):
        out[...] = held[(y + t) % NX]
    c, s = cos[...], sin[...]
    for h in range(GROUP):
        q_ref[h * TOK : (h + 1) * TOK, :] = turn(total[:, h * HD : (h + 1) * HD], c, s).astype(bf16)
    kv_ref[0:TOK, :] = turn(total[:, 512:640], c, s).astype(bf16)
    kv_ref[TOK:, :] = total[:, 640:768].astype(bf16)


def block_start(sc, row):
    start = 0
    for d in range(8):
        start = jnp.maximum(start, jnp.where(sc[8 + d] <= row, sc[8 + d], 0))
    return start


def query_rows(sc, visit):
    first = ((sc[1] + visit) * NZ * NC + sc[2] * NC + sc[3]) * TOK
    rows = first + lax.broadcasted_iota(i32, (1, QW), 1) % TOK
    starts = jnp.zeros((1, QW), i32)
    for d in range(8):
        starts = jnp.maximum(starts, jnp.where(rows >= sc[8 + d], sc[8 + d], 0))
    return first, rows, starts


def key_tile(sc, s):
    return sc[1] * NZ + (sc[2] + NZ - s) % NZ


def tile_needed(sc, visit, s):
    pair = key_tile(sc, s)
    first = ((sc[1] + visit) * NZ * NC + sc[2] * NC + sc[3]) * TOK
    live = (sc[1] + visit < NY) & (pair <= (sc[1] + visit) * NZ + sc[2])
    return live & (pair * 256 + 255 >= block_start(sc, first))


def load_keys(kvs, keys, values):
    for s in range(NZ):
        for e in range(NC):
            block = kvs[e * NZ + s]
            keys[s, e * TOK : (e + 1) * TOK, :] = block[0:TOK, :]
            values[s, e * TOK : (e + 1) * TOK, :] = block[TOK:, :]


def tile_mask(sc, s, rows, starts):
    offset = lax.broadcasted_iota(i32, (2 * TOK, QW), 0) ^ (sc[3] * TOK)
    key_rows = key_tile(sc, s) * 256 + offset
    return (key_rows >= starts) & (key_rows <= rows)


def forward_kernel(sc, *refs):
    qs, dos, kvs = refs[0:3], refs[3:6], refs[6:22]
    outs, stats = refs[22:25], refs[25]
    keys, values, acc, top, total = refs[26:]
    load_keys(kvs, keys, values)
    stats[...] = jnp.zeros_like(stats)
    for visit in range(VISITS):
        q_ref = qs[visit]
        _, rows, starts = query_rows(sc, visit)
        acc[...] = jnp.zeros_like(acc)
        total[...] = jnp.zeros_like(total)
        top[...] = jnp.full_like(top, masked)

        @pl.loop(0, NZ)
        def _(s):
            @pl.when(tile_needed(sc, visit, s))
            def _():
                scores = dot(keys[s], q_ref[...], NT) * (scale * log2e)
                scores = jnp.where(tile_mask(sc, s, rows, starts), scores, masked)
                old = top[...]
                new = jnp.maximum(old, jnp.max(scores, axis=0, keepdims=True))
                base = jnp.maximum(new, 0.1 * masked)
                p = jnp.exp2(scores - base)
                fade = jnp.exp2(old - base)
                top[...] = new
                total[...] = total[...] * fade + jnp.sum(p, axis=0, keepdims=True)
                acc[...] = acc[...] * fade + dot(values[s], p.astype(bf16), TN)

        mass = total[...]
        some = mass > 0.0
        mass = jnp.where(some, mass, 1.0)
        out = acc[...] * (1.0 / mass)
        outs[visit][...] = out.astype(bf16)
        stats[visit : visit + 1, :] = jnp.where(some, top[...] + jnp.log2(mass), masked)
        delta = jnp.sum(dos[visit][...].astype(f32).T * out, axis=0, keepdims=True)
        stats[4 + visit : 5 + visit, :] = delta


def combine_stats(sc, visit, held):
    logs, deltas = [], []
    for j in range(VISITS):
        t = visit - j
        logs.append(jnp.where(sc[1] + t >= 0, held[t % NY][j : j + 1, :], masked))
        deltas.append(held[t % NY][4 + j : 5 + j, :])
    top = functools.reduce(jnp.maximum, logs)
    weights = [jnp.exp2(v - top) for v in logs]
    mass = sum(weights)
    weights = [v / mass for v in weights]
    return top + jnp.log2(mass), sum(a * b for a, b in zip(weights, deltas)), weights


def backward_kernel(sc, *refs):
    qs, dos, kvs, held = refs[0:3], refs[3:6], refs[6:22], refs[22:26]
    dqs, own_ref, other_ref = refs[26:29], refs[29], refs[30]
    keys, values, q_all, do_all, dq_acc, logs, deltas, dk, dv = refs[31:]
    load_keys(kvs, keys, values)
    dq_acc[...] = jnp.zeros_like(dq_acc)
    for visit in range(VISITS):
        q_all[visit] = qs[visit][...]
        do_all[visit] = dos[visit][...]
        log_total, delta, _ = combine_stats(sc, visit, held)
        logs[visit] = log_total
        deltas[visit] = delta

    @pl.loop(0, NZ)
    def _(s):
        dk[...] = jnp.zeros_like(dk)
        dv[...] = jnp.zeros_like(dv)

        @pl.loop(0, VISITS)
        def _(visit):
            @pl.when(tile_needed(sc, visit, s))
            def _():
                _, rows, starts = query_rows(sc, visit)
                q, do = q_all[visit], do_all[visit]
                scores = dot(keys[s], q, NT) * (scale * log2e) - logs[visit]
                p = jnp.exp2(jnp.where(tile_mask(sc, s, rows, starts), scores, masked))
                dp = dot(values[s], do, NT)
                ds = (p * (dp - deltas[visit])).astype(bf16)
                dv[...] += dot(p.astype(bf16), do)
                dk[...] += dot(ds, q)
                dq_acc[visit] += dot(keys[s], ds, TN)

        for e, out in enumerate((own_ref, other_ref)):
            half = slice(e * TOK, (e + 1) * TOK)
            out[s, 0:TOK, :] = (dk[half, :] * scale).astype(bf16)
            out[s, TOK:, :] = dv[half, :].astype(bf16)

    for visit in range(VISITS):
        dqs[visit][...] = (dq_acc[visit] * scale).astype(bf16)


def context_kernel(sc, o0, o1, o2, s0, s1, s2, s3, mh, send_ref, rows):
    _, _, weights = combine_stats(sc, 0, (s0, s1, s2, s3))
    out = o0[...].astype(f32) * weights[0]
    for j, o in ((1, o1), (2, o2)):
        out = out + jnp.where(sc[1] >= j, o[...].astype(f32), 0.0) * weights[j]
    for h in range(GROUP):
        rows[:, h * HD : (h + 1) * HD] = out[:, h * TOK : (h + 1) * TOK].T.astype(bf16)
    send_ref[...] = dot(mh[...], rows[...]).astype(bf16)


def add_split_kernel(own, came, *outs):
    for s in range(NZ):
        outs[s][...] = (own[s].astype(f32) + came[s].astype(f32)).astype(bf16)


def rows_kernel(sc, *refs):
    parts, dqs, (cos, sin, w), hids = refs[0:8], refs[8:11], refs[11:14], refs[14:18]
    rg_ref, keep_ref, inner_ref = refs[18], refs[19], refs[20]
    sends = refs[21:24]
    x = sc[4]
    c, s = cos[...], sin[...]
    dq = dqs[0][...].astype(f32)
    for j in (1, 2):
        dq = dq + jnp.where(sc[1] >= j, dqs[j][...].astype(f32), 0.0)
    for h in range(GROUP):
        rg_ref[:, h * HD : (h + 1) * HD] = turn_back(dq[:, h * TOK : (h + 1) * TOK].T, c, s).astype(bf16)
    dkv = sum(p[...].astype(f32) for p in parts)
    rg_ref[:, 512:640] = turn_back(dkv[0:TOK], c, s).astype(bf16)
    rg_ref[:, 640:768] = dkv[TOK:].astype(bf16)
    rg = rg_ref[...]
    inner = jnp.zeros((TOK, 1), f32)
    for t in range(NX):
        chunk = (x + t) % NX
        part = dot(rg, w[pl.ds(pl.multiple_of(chunk * 512, 512), 512), :], NT)
        inner = inner + jnp.sum(part * hids[-t % NX][...].astype(f32), axis=1, keepdims=True)
        if t == 0:
            keep_ref[...] = part
        else:
            sends[t - 1][0:TOK, :] = part.astype(bf16)
    row = jnp.broadcast_to(inner, (TOK, TOK)).T[0:16, :]
    inner_ref[...] = row[0:8, :]
    high = row.astype(bf16).astype(f32)
    line = lax.broadcasted_iota(i32, (16, TOK), 0)
    both = jnp.where(line == 0, high, jnp.where(line == 1, row - high, 0.0)).astype(bf16)
    for out in sends:
        out[TOK:, :] = jnp.concatenate([both, jnp.zeros((16, 384), bf16)], axis=1)


def input_kernel(keep, inner, r1, r2, r3, inv_ref, hid, out_ref):
    total = keep[...]
    row = inner[0:1, :]
    for r in (r1, r2, r3):
        total = total + r[0:TOK, :].astype(f32)
        tail = r[TOK:, 0:TOK].astype(f32)
        row = row + tail[0:1, :] + tail[1:2, :]
    column = jnp.broadcast_to(row, (TOK, TOK)).T[:, 0:1]
    inv = inv_ref[:, 0:1]
    out_ref[...] = inv * total - hid[...].astype(f32) * (inv * inv * inv * column * (1.0 / (NX * 512)))


def weight_kernel(sc, *refs):
    ns, rgs, own_ref, other_ref = refs[0:4], refs[4:8], refs[8], refs[9]
    n_all, rg_all, product = refs[10:]
    for t in range(NY):
        n_all[t * TOK : (t + 1) * TOK, :] = ns[t][...]
        rg_all[t * TOK : (t + 1) * TOK, :] = rgs[t][...]
    product[...] = dot(n_all[...], rg_all[...], TN)
    z, core = sc[2], sc[3]
    for s in range(NZ):
        first = ((z + s) % NZ) * 64
        own_ref[s] = product[pl.ds(pl.multiple_of(first + core * 32, 32), 32), :].astype(bf16)
        other_ref[s] = product[pl.ds(pl.multiple_of(first + (1 - core) * 32, 32), 32), :].astype(bf16)


def sum_kernel(*refs):
    refs[-1][...] = sum(r[...].astype(f32) for r in refs[:-1])


def index_of(y, z, c):
    return (y * NZ + z) * NC + c


def over_y(a, shift, wrap=True):
    pairs = [
        (index_of(y, z, c), index_of((y + shift) % NY, z, c))
        for y in range(NY)
        for z in range(NZ)
        for c in range(NC)
        if wrap or 0 <= y + shift < NY
    ]
    return lax.ppermute(a, "ctx", pairs)


def over_z(a, shift):
    pairs = [
        (index_of(y, z, c), index_of(y, (z + shift) % NZ, c))
        for y in range(NY)
        for z in range(NZ)
        for c in range(NC)
    ]
    return lax.ppermute(a, "ctx", pairs)


def over_c(a):
    pairs = [(index_of(y, z, c), index_of(y, z, 1 - c)) for y in range(NY) for z in range(NZ) for c in range(NC)]
    return lax.ppermute(a, "ctx", pairs)


def over_x(a, shift):
    return lax.ppermute(a, "fsdp", [(x, (x + shift) % NX) for x in range(NX)])


def exchange_slots(send):
    width = send.shape[1]
    came = lax.all_to_all(send.reshape(N_CTX, CAP, width), "ctx", split_axis=0, concat_axis=0, tiled=True)
    return came.reshape(SLOTS, width)


def shards(hidden, w, doc_lengths, owners, context_grad):
    me = lax.axis_index("ctx").astype(i32)
    x = lax.axis_index("fsdp").astype(i32)
    doc_starts = (jnp.cumsum(doc_lengths) - doc_lengths).astype(i32)
    zero = jnp.zeros((), i32)
    sc = jnp.concatenate(
        [jnp.stack([me, me // (NZ * NC), me // NC % NZ, me % NC, x, zero, zero, zero]), doc_starts]
    )
    hids = [hidden] + [over_x(hidden, s) for s in range(1, NX)]

    mo, mh, send = call(
        route_kernel,
        [((SLOTS, TOK), bf16), ((SLOTS, TOK), bf16), ((SLOTS, QW), bf16)],
        "svv",
        (sc, owners.reshape(N_CTX, TOK), context_grad),
        name="route",
    )
    arrived = exchange_slots(send)

    home = me * TOK + jnp.arange(TOK, dtype=i32)
    start = jnp.max(jnp.where(home[:, None] >= doc_starts[None, :], doc_starts[None, :], 0), axis=1)
    frequency = rope_base ** (-(2.0 * jnp.arange(HD // 2, dtype=f32)) / HD)
    angles = (home - start).astype(f32)[:, None] * frequency[None, :]
    cos, sin = jnp.cos(angles), jnp.sin(angles)
    cos, sin = jnp.concatenate([cos, cos], axis=1), jnp.concatenate([-sin, sin], axis=1)

    q, kv, n0, n1, n2, n3, inv = call(
        project_kernel,
        [((QW, HD), bf16), ((2 * TOK, HD), bf16)] + [((TOK, 512), bf16)] * 4 + [((TOK, HD), f32)],
        "svvvvvvv",
        (sc, *hids, w, cos, sin),
        scratch=[pltpu.VMEM((NX, TOK, 512), bf16)],
        flops=4 * 10**8,
        moved=4 * 10**6,
        name="project",
    )
    kv_own = [kv] + [over_z(kv, s) for s in range(1, NZ)]
    qs = [q, over_y(q, -1, False), over_y(q, -2, False)]
    kv_other = [over_c(a) for a in kv_own]
    kvs = kv_own + kv_other
    ns = [n0] + [over_y(n, t) for t, n in ((1, n1), (2, n2), (3, n3))]

    (do,) = call(grad_home_kernel, [((QW, HD), bf16)], "vv", (mh, arrived), name="grad_home")
    dos = [do, over_y(do, -1, False), over_y(do, -2, False)]

    *outs, stats = call(
        forward_kernel,
        [((HD, QW), bf16)] * 3 + [((8, QW), f32)],
        "s" + "v" * 22,
        (sc, *qs, *dos, *kvs),
        scratch=[
            pltpu.VMEM((NZ, 2 * TOK, HD), bf16),
            pltpu.VMEM((NZ, 2 * TOK, HD), bf16),
            pltpu.VMEM((HD, QW), f32),
            pltpu.VMEM((1, QW), f32),
            pltpu.VMEM((1, QW), f32),
        ],
        flops=3 * 10**9,
        name="forward",
    )
    held = [stats] + [over_y(stats, -t) for t in (1, 2, 3)]
    o_came = [outs[0], over_y(outs[1], 1, False), over_y(outs[2], 2, False)]

    *dqs, dkv_own, dkv_other = call(
        backward_kernel,
        [((HD, QW), bf16)] * 3 + [((NZ, 2 * TOK, HD), bf16)] * 2,
        "s" + "v" * 26,
        (sc, *qs, *dos, *kvs, *held),
        scratch=[
            pltpu.VMEM((NZ, 2 * TOK, HD), bf16),
            pltpu.VMEM((NZ, 2 * TOK, HD), bf16),
            pltpu.VMEM((VISITS, QW, HD), bf16),
            pltpu.VMEM((VISITS, QW, HD), bf16),
            pltpu.VMEM((VISITS, HD, QW), f32),
            pltpu.VMEM((VISITS, 1, QW), f32),
            pltpu.VMEM((VISITS, 1, QW), f32),
            pltpu.VMEM((2 * TOK, HD), f32),
            pltpu.VMEM((2 * TOK, HD), f32),
        ],
        flops=5 * 10**9,
        name="backward",
    )
    dkv_came = over_c(dkv_other)
    dq_came = [dqs[0], over_y(dqs[1], 1, False), over_y(dqs[2], 2, False)]

    (context_send,) = call(
        context_kernel,
        [((SLOTS, QW), bf16)],
        "s" + "v" * 8,
        (sc, *o_came, *held, mh),
        scratch=[pltpu.VMEM((TOK, QW), bf16)],
        name="context",
    )
    context_came = exchange_slots(context_send)

    dkv_parts = call(
        add_split_kernel, [((2 * TOK, HD), bf16)] * NZ, "vv", (dkv_own, dkv_came), name="add_dkv"
    )
    dkv_home = [dkv_parts[0]] + [over_z(dkv_parts[s], -s) for s in range(1, NZ)]

    rg, keep, inner, *sends = call(
        rows_kernel,
        [((TOK, 768), bf16), ((TOK, 512), f32), ((8, TOK), f32)] + [((TOK + 16, 512), bf16)] * 3,
        "s" + "v" * 18,
        (sc, *dkv_home, *dq_came, cos, sin, w, *hids),
        flops=4 * 10**8,
        moved=4 * 10**6,
        name="rows",
    )
    rgs = [rg] + [over_y(rg, t) for t in (1, 2, 3)]
    totals = [over_x(a, t) for t, a in zip((1, 2, 3), sends)]
    w_own, w_other = call(
        weight_kernel,
        [((NZ, 32, 768), bf16)] * 2,
        "s" + "v" * 8,
        (sc, *ns, *rgs),
        scratch=[
            pltpu.VMEM((NY * TOK, 512), bf16),
            pltpu.VMEM((NY * TOK, 768), bf16),
            pltpu.VMEM((512, 768), f32),
        ],
        flops=4 * 10**8,
        name="weight",
    )
    w_came = over_c(w_other)
    (input_grad,) = call(
        input_kernel,
        [((TOK, 512), f32)],
        "v" * 7,
        (keep, inner, *totals, inv, hidden),
        name="input",
    )
    (context,) = call(place_kernel, [((TOK, QW), bf16)], "vv", (mo, context_came), name="place")
    w_parts = call(add_split_kernel, [((32, 768), bf16)] * NZ, "vv", (w_own, w_came), name="add_weight")
    w_home = [w_parts[0]] + [over_z(w_parts[s], s) for s in range(1, NZ)]
    (weight_grad,) = call(sum_kernel, [((32, 768), f32)], "v" * NZ, w_home, name="sum_weight")
    return context, input_grad, weight_grad


def solution(mesh):
    placed = (P("ctx", "fsdp"), P(None, "fsdp"), P(), P(), P("ctx", "fsdp"))
    return jax.shard_map(
        shards,
        mesh=mesh,
        in_specs=placed,
        out_specs=(P("ctx", "fsdp"), P("ctx", "fsdp"), P("ctx", "fsdp")),
        check_vma=False,
    )
```

```python
import functools

import jax
import jax.numpy as jnp
from jax import lax
from jax.experimental import pallas as pl
from jax.experimental.pallas import tpu as pltpu
from jax.sharding import PartitionSpec as P

HD = 128
GROUP = 4
TOK = 128
NY, NZ, NC = 4, 8, 2
N_CTX = NY * NZ * NC
NX = 4
CAP = 4
SLOTS = N_CTX * CAP
VISITS = 3
KEPT = (0, 3, 5)
FROM_BELOW = (1, 4, 6)
FROM_ABOVE = (7, 2)
QW = GROUP * TOK
epsilon = 1e-05
rope_base = 500000.0
scale = HD ** (-0.5)
log2e = 1.4426950408889634
masked = -1e30

f32, bf16, i32 = jnp.float32, jnp.bfloat16, jnp.int32

NT = (((1,), (1,)), ((), ()))
NN = (((1,), (0,)), ((), ()))
TN = (((0,), (0,)), ((), ()))


def dot(a, b, dims=NN):
    return lax.dot_general(a, b, dims, preferred_element_type=f32)


def call(kernel, outs, in_kinds, args, scratch=(), flops=10**8, moved=2 * 10**6, name=None):
    vm = pl.BlockSpec(memory_space=pltpu.VMEM)
    sm = pl.BlockSpec(memory_space=pltpu.SMEM)
    return pl.pallas_call(
        kernel,
        out_shape=[jax.ShapeDtypeStruct(s, d) for s, d in outs],
        in_specs=[sm if k == "s" else vm for k in in_kinds],
        out_specs=[vm] * len(outs),
        scratch_shapes=list(scratch),
        compiler_params=pltpu.CompilerParams(vmem_limit_bytes=48 * 1024 * 1024),
        cost_estimate=pl.CostEstimate(flops=flops, bytes_accessed=moved, transcendentals=0),
        name=name,
    )(*args)


def route_kernel(sc, owners, cg, mo_ref, mh_ref, send_ref):
    me = sc[0]
    mine = (owners[...] == me).astype(f32).astype(bf16)
    count = dot(mine, jnp.ones((TOK, TOK), bf16)).astype(bf16)
    slot_src = lax.broadcasted_iota(i32, (SLOTS, N_CTX), 0) // CAP
    source = lax.broadcasted_iota(i32, (SLOTS, N_CTX), 1)
    base = dot((source < slot_src).astype(f32).astype(bf16), count)
    here = dot((source == slot_src).astype(f32).astype(bf16), count)
    slot = lax.broadcasted_iota(i32, (SLOTS, TOK), 0)
    place = lax.broadcasted_iota(i32, (SLOTS, TOK), 1)
    rank = (slot % CAP).astype(f32)
    mo = jnp.where((base + rank == place.astype(f32)) & (rank < here), 1.0, 0.0).astype(bf16)
    mo_ref[...] = mo
    send_ref[...] = dot(mo, cg[...]).astype(bf16)
    own = jnp.broadcast_to(owners[pl.ds(me, 1), :].astype(f32), (TOK, TOK))
    earlier = lax.broadcasted_iota(i32, (TOK, TOK), 0) < lax.broadcasted_iota(i32, (TOK, TOK), 1)
    same = jnp.where((own == own.T) & earlier, 1.0, 0.0)
    home_slot = own[0:1, :] * CAP + jnp.sum(same, axis=0, keepdims=True)
    mh_ref[...] = jnp.where(slot.astype(f32) == home_slot, 1.0, 0.0).astype(bf16)


def grad_home_kernel(mh, arrived, out_ref):
    rows = dot(mh[...], arrived[...], TN).astype(bf16)
    for h in range(GROUP):
        out_ref[h * TOK : (h + 1) * TOK, :] = rows[:, h * HD : (h + 1) * HD]


def place_kernel(mo, arrived, out_ref):
    out_ref[...] = dot(mo[...], arrived[...], TN).astype(bf16)


def turn(t, c, s):
    return t * c + pltpu.roll(t, HD // 2, 1) * s


def turn_back(t, c, s):
    return t * c - pltpu.roll(t, HD // 2, 1) * s


def project_kernel(sc, h0, h1, h2, h3, w, cos, sin, q_ref, kv_ref, n0, n1, n2, n3, inv_ref, held):
    y, x = sc[1], sc[4]
    blocks = [h[...].astype(f32) for h in (h0, h1, h2, h3)]
    square = sum(jnp.sum(b * b, axis=1, keepdims=True) for b in blocks)
    inv = lax.rsqrt(square * (1.0 / (NX * 512)) + epsilon)
    inv_ref[...] = jnp.broadcast_to(inv, (TOK, HD))
    total = jnp.zeros((TOK, 768), f32)
    for s in range(NX):
        chunk = (x + NX - s) % NX
        normed = (blocks[s] * inv).astype(bf16)
        held[chunk] = normed
        total = total + dot(normed, w[pl.ds(pl.multiple_of(chunk * 512, 512), 512), :])
    for t, out in enumerate((n0, n1, n2, n3)):
        out[...] = held[(y + t) % NX]
    c, s = cos[...], sin[...]
    for h in range(GROUP):
        q_ref[h * TOK : (h + 1) * TOK, :] = turn(total[:, h * HD : (h + 1) * HD], c, s).astype(bf16)
    kv_ref[0:TOK, :] = turn(total[:, 512:640], c, s).astype(bf16)
    kv_ref[TOK:, :] = total[:, 640:768].astype(bf16)


def block_start(sc, row):
    start, begin = 0, sc[8]
    for d in range(1, 8):
        start = jnp.where(begin <= row, begin, start)
        begin = begin + sc[8 + d]
    return start


def query_rows(sc, visit):
    first = ((sc[1] + visit) * NZ * NC + sc[2] * NC + sc[3]) * TOK
    rows = first + lax.broadcasted_iota(i32, (1, QW), 1) % TOK
    starts, begin = jnp.zeros((1, QW), i32), sc[8]
    for d in range(1, 8):
        starts = jnp.where(rows >= begin, begin, starts)
        begin = begin + sc[8 + d]
    return first, rows, starts


def key_tile(sc, s):
    return sc[1] * NZ + (sc[2] + NZ - s) % NZ


def tile_needed(sc, visit, s):
    pair = key_tile(sc, s)
    first = ((sc[1] + visit) * NZ * NC + sc[2] * NC + sc[3]) * TOK
    live = (sc[1] + visit < NY) & (pair <= (sc[1] + visit) * NZ + sc[2])
    return live & (pair * 256 + 255 >= block_start(sc, first))


def load_keys(kvs, keys, values):
    for e in range(NC):
        for stack, steps in zip(kvs[3 * e : 3 * e + 3], (KEPT, FROM_BELOW, FROM_ABOVE)):
            for i, s in enumerate(steps):
                keys[s, e * TOK : (e + 1) * TOK, :] = stack[i, 0:TOK, :]
                values[s, e * TOK : (e + 1) * TOK, :] = stack[i, TOK:, :]


def pack_kernel(b0, b3, b5, three_ref, two_ref):
    for i, b in enumerate((b0, b3, b5)):
        three_ref[i] = b[...]
        if i < 2:
            two_ref[i] = b[...]


def tile_mask(sc, s, rows, starts):
    offset = lax.broadcasted_iota(i32, (2 * TOK, QW), 0) ^ (sc[3] * TOK)
    key_rows = key_tile(sc, s) * 256 + offset
    return (key_rows >= starts) & (key_rows <= rows)


def forward_kernel(sc, *refs):
    qs, dos, kvs = refs[0:3], refs[3:6], refs[6:12]
    outs, stats = refs[12:15], refs[15]
    keys, values, acc, top, total = refs[16:]
    load_keys(kvs, keys, values)
    stats[...] = jnp.zeros_like(stats)
    for visit in range(VISITS):
        q_ref = qs[visit]
        _, rows, starts = query_rows(sc, visit)
        acc[...] = jnp.zeros_like(acc)
        total[...] = jnp.zeros_like(total)
        top[...] = jnp.full_like(top, masked)

        @pl.loop(0, NZ)
        def _(s):
            @pl.when(tile_needed(sc, visit, s))
            def _():
                scores = dot(keys[s], q_ref[...], NT) * (scale * log2e)
                scores = jnp.where(tile_mask(sc, s, rows, starts), scores, masked)
                old = top[...]
                new = jnp.maximum(old, jnp.max(scores, axis=0, keepdims=True))
                base = jnp.maximum(new, 0.1 * masked)
                p = jnp.exp2(scores - base)
                fade = jnp.exp2(old - base)
                top[...] = new
                total[...] = total[...] * fade + jnp.sum(p, axis=0, keepdims=True)
                acc[...] = acc[...] * fade + dot(values[s], p.astype(bf16), TN)

        mass = total[...]
        some = mass > 0.0
        mass = jnp.where(some, mass, 1.0)
        out = acc[...] * (1.0 / mass)
        outs[visit][...] = out.astype(bf16)
        stats[visit : visit + 1, :] = jnp.where(some, top[...] + jnp.log2(mass), masked)
        delta = jnp.sum(dos[visit][...].astype(f32).T * out, axis=0, keepdims=True)
        stats[4 + visit : 5 + visit, :] = delta


def combine_stats(sc, visit, held):
    logs, deltas = [], []
    for j in range(VISITS):
        t = visit - j
        logs.append(jnp.where(sc[1] + t >= 0, held[t % NY][j : j + 1, :], masked))
        deltas.append(held[t % NY][4 + j : 5 + j, :])
    top = functools.reduce(jnp.maximum, logs)
    weights = [jnp.exp2(v - top) for v in logs]
    mass = sum(weights)
    weights = [v / mass for v in weights]
    return top + jnp.log2(mass), sum(a * b for a, b in zip(weights, deltas)), weights


def backward_kernel(sc, *refs):
    qs, dos, kvs, held = refs[0:3], refs[3:6], refs[6:12], refs[12:16]
    dqs, own_ref, other_ref = refs[16:19], refs[19], refs[20]
    keys, values, q_all, do_all, dq_acc, logs, deltas, dk, dv = refs[21:]
    load_keys(kvs, keys, values)
    dq_acc[...] = jnp.zeros_like(dq_acc)
    for visit in range(VISITS):
        q_all[visit] = qs[visit][...]
        do_all[visit] = dos[visit][...]
        log_total, delta, _ = combine_stats(sc, visit, held)
        logs[visit] = log_total
        deltas[visit] = delta

    @pl.loop(0, NZ)
    def _(s):
        dk[...] = jnp.zeros_like(dk)
        dv[...] = jnp.zeros_like(dv)

        @pl.loop(0, VISITS)
        def _(visit):
            @pl.when(tile_needed(sc, visit, s))
            def _():
                _, rows, starts = query_rows(sc, visit)
                q, do = q_all[visit], do_all[visit]
                scores = dot(keys[s], q, NT) * (scale * log2e) - logs[visit]
                p = jnp.exp2(jnp.where(tile_mask(sc, s, rows, starts), scores, masked))
                dp = dot(values[s], do, NT)
                ds = (p * (dp - deltas[visit])).astype(bf16)
                dv[...] += dot(p.astype(bf16), do)
                dk[...] += dot(ds, q)
                dq_acc[visit] += dot(keys[s], ds, TN)

        for e, out in enumerate((own_ref, other_ref)):
            half = slice(e * TOK, (e + 1) * TOK)
            out[s, 0:TOK, :] = (dk[half, :] * scale).astype(bf16)
            out[s, TOK:, :] = dv[half, :].astype(bf16)

    for visit in range(VISITS):
        dqs[visit][...] = (dq_acc[visit] * scale).astype(bf16)


def context_kernel(sc, o0, o1, o2, s0, s1, s2, s3, mh, send_ref, rows):
    _, _, weights = combine_stats(sc, 0, (s0, s1, s2, s3))
    out = o0[...].astype(f32) * weights[0]
    for j, o in ((1, o1), (2, o2)):
        out = out + jnp.where(sc[1] >= j, o[...].astype(f32), 0.0) * weights[j]
    for h in range(GROUP):
        rows[:, h * HD : (h + 1) * HD] = out[:, h * TOK : (h + 1) * TOK].T.astype(bf16)
    send_ref[...] = dot(mh[...], rows[...]).astype(bf16)


def add_cores_kernel(own, came, kept, below, above):
    for out, steps in ((kept, KEPT), (below, FROM_BELOW), (above, FROM_ABOVE)):
        for i, s in enumerate(steps):
            out[i] = (own[s].astype(f32) + came[s].astype(f32)).astype(out.dtype)


def add_near_kernel(kept, below, above, o0, o3, o5):
    o0[...] = kept[0] + below[0].astype(f32) + above[0].astype(f32)
    o3[...] = (kept[1] + below[1].astype(f32) + above[1].astype(f32)).astype(bf16)
    o5[...] = (kept[2] + below[2].astype(f32)).astype(bf16)


def rows_kernel(sc, *refs):
    parts, dqs, (cos, sin, w), hids = refs[0:3], refs[3:6], refs[6:9], refs[9:13]
    rg_ref, keep_ref, inner_ref = refs[13], refs[14], refs[15]
    sends = refs[16:19]
    x = sc[4]
    c, s = cos[...], sin[...]
    dq = dqs[0][...].astype(f32)
    for j in (1, 2):
        dq = dq + jnp.where(sc[1] >= j, dqs[j][...].astype(f32), 0.0)
    for h in range(GROUP):
        rg_ref[:, h * HD : (h + 1) * HD] = turn_back(dq[:, h * TOK : (h + 1) * TOK].T, c, s).astype(bf16)
    dkv = sum(p[...].astype(f32) for p in parts)
    rg_ref[:, 512:640] = turn_back(dkv[0:TOK], c, s).astype(bf16)
    rg_ref[:, 640:768] = dkv[TOK:].astype(bf16)
    rg = rg_ref[...]
    inner = jnp.zeros((TOK, 1), f32)
    for t in range(NX):
        chunk = (x + t) % NX
        part = dot(rg, w[pl.ds(pl.multiple_of(chunk * 512, 512), 512), :], NT)
        inner = inner + jnp.sum(part * hids[-t % NX][...].astype(f32), axis=1, keepdims=True)
        if t == 0:
            keep_ref[...] = part
        else:
            sends[t - 1][0:TOK, :] = part.astype(bf16)
    row = jnp.broadcast_to(inner, (TOK, TOK)).T[0:16, :]
    inner_ref[...] = row[0:8, :]
    high = row.astype(bf16).astype(f32)
    line = lax.broadcasted_iota(i32, (16, TOK), 0)
    both = jnp.where(line == 0, high, jnp.where(line == 1, row - high, 0.0)).astype(bf16)
    for out in sends:
        out[TOK:, :] = jnp.concatenate([both, jnp.zeros((16, 384), bf16)], axis=1)


def input_kernel(keep, inner, r1, r2, r3, inv_ref, hid, out_ref):
    total = keep[...]
    row = inner[0:1, :]
    for r in (r1, r2, r3):
        total = total + r[0:TOK, :].astype(f32)
        tail = r[TOK:, 0:TOK].astype(f32)
        row = row + tail[0:1, :] + tail[1:2, :]
    column = jnp.broadcast_to(row, (TOK, TOK)).T[:, 0:1]
    inv = inv_ref[:, 0:1]
    out_ref[...] = inv * total - hid[...].astype(f32) * (inv * inv * inv * column * (1.0 / (NX * 512)))


def weight_kernel(sc, *refs):
    ns, rgs, own_ref, other_ref = refs[0:4], refs[4:8], refs[8], refs[9]
    n_all, rg_all, product = refs[10:]
    for t in range(NY):
        n_all[t * TOK : (t + 1) * TOK, :] = ns[t][...]
        rg_all[t * TOK : (t + 1) * TOK, :] = rgs[t][...]
    product[...] = dot(n_all[...], rg_all[...], TN)
    z, core = sc[2], sc[3]
    for s in range(NZ):
        first = ((z + NZ - s) % NZ) * 64
        own_ref[s] = product[pl.ds(pl.multiple_of(first + core * 32, 32), 32), :].astype(bf16)
        other_ref[s] = product[pl.ds(pl.multiple_of(first + (1 - core) * 32, 32), 32), :].astype(bf16)


def sum_kernel(*refs):
    refs[-1][...] = sum(r[...].astype(f32) for r in refs[:-1])


def index_of(y, z, c):
    return (y * NZ + z) * NC + c


def over_y(a, shift, wrap=True):
    pairs = [
        (index_of(y, z, c), index_of((y + shift) % NY, z, c))
        for y in range(NY)
        for z in range(NZ)
        for c in range(NC)
        if wrap or 0 <= y + shift < NY
    ]
    return lax.ppermute(a, "ctx", pairs)


def over_z(a, shift):
    pairs = [
        (index_of(y, z, c), index_of(y, (z + shift) % NZ, c))
        for y in range(NY)
        for z in range(NZ)
        for c in range(NC)
    ]
    return lax.ppermute(a, "ctx", pairs)


def over_c(a):
    pairs = [(index_of(y, z, c), index_of(y, z, 1 - c)) for y in range(NY) for z in range(NZ) for c in range(NC)]
    return lax.ppermute(a, "ctx", pairs)


def over_x(a, shift):
    return lax.ppermute(a, "fsdp", [(x, (x + shift) % NX) for x in range(NX)])


def exchange_slots(send):
    width = send.shape[1]
    came = lax.all_to_all(send.reshape(N_CTX, CAP, width), "ctx", split_axis=0, concat_axis=0, tiled=True)
    return came.reshape(SLOTS, width)


def reduce_cores_and_z(own, other, name):
    shape = own.shape[1:]
    came = over_c(other)
    kept, below, above = call(
        add_cores_kernel,
        [((3,) + shape, f32), ((3,) + shape, bf16), ((2,) + shape, bf16)],
        "vv",
        (own, came),
        name="add_cores_" + name,
    )
    below, above = over_z(below, -1), over_z(above, 1)
    o0, o3, o5 = call(
        add_near_kernel,
        [(shape, f32), (shape, bf16), (shape, bf16)],
        "vvv",
        (kept, below, above),
        name="add_near_" + name,
    )
    return o0, over_z(o3, -3), over_z(o5, 3)


def shards(hidden, w, doc_lengths, owners, context_grad):
    me = lax.axis_index("ctx").astype(i32)
    x = lax.axis_index("fsdp").astype(i32)
    zero = jnp.zeros((), i32)
    sc = jnp.concatenate(
        [jnp.stack([me, me // (NZ * NC), me // NC % NZ, me % NC, x, zero, zero, zero]), doc_lengths.astype(i32)]
    )
    hids = [hidden] + [over_x(hidden, s) for s in range(1, NX)]

    mo, mh, send = call(
        route_kernel,
        [((SLOTS, TOK), bf16), ((SLOTS, TOK), bf16), ((SLOTS, QW), bf16)],
        "svv",
        (sc, owners.reshape(N_CTX, TOK), context_grad),
        name="route",
    )
    arrived = exchange_slots(send)

    home = me * TOK + jnp.arange(TOK, dtype=i32)
    docs = jnp.arange(8, dtype=i32)
    doc_starts = jnp.sum(jnp.where(docs[:, None] > docs[None, :], doc_lengths[None, :], 0), axis=1)
    start = jnp.max(jnp.where(home[:, None] >= doc_starts[None, :], doc_starts[None, :], 0), axis=1)
    frequency = rope_base ** (-(2.0 * jnp.arange(HD // 2, dtype=f32)) / HD)
    angles = (home - start).astype(f32)[:, None] * frequency[None, :]
    cos, sin = jnp.cos(angles), jnp.sin(angles)
    cos, sin = jnp.concatenate([cos, cos], axis=1), jnp.concatenate([-sin, sin], axis=1)

    q, kv, n0, n1, n2, n3, inv = call(
        project_kernel,
        [((QW, HD), bf16), ((2 * TOK, HD), bf16)] + [((TOK, 512), bf16)] * 4 + [((TOK, HD), f32)],
        "svvvvvvv",
        (sc, *hids, w, cos, sin),
        scratch=[pltpu.VMEM((NX, TOK, 512), bf16)],
        flops=4 * 10**8,
        moved=4 * 10**6,
        name="project",
    )
    three, two = call(
        pack_kernel,
        [((3, 2 * TOK, HD), bf16), ((2, 2 * TOK, HD), bf16)],
        "vvv",
        (kv, over_z(kv, 3), over_z(kv, -3)),
        name="pack",
    )
    kv_own = [three, over_z(three, 1), over_z(two, -1)]
    qs = [q, over_y(q, -1, False), over_y(q, -2, False)]
    kvs = kv_own + [over_c(a) for a in kv_own]
    ns = [n0] + [over_y(n, t) for t, n in ((1, n1), (2, n2), (3, n3))]

    (do,) = call(grad_home_kernel, [((QW, HD), bf16)], "vv", (mh, arrived), name="grad_home")
    dos = [do, over_y(do, -1, False), over_y(do, -2, False)]

    *outs, stats = call(
        forward_kernel,
        [((HD, QW), bf16)] * 3 + [((8, QW), f32)],
        "s" + "v" * 12,
        (sc, *qs, *dos, *kvs),
        scratch=[
            pltpu.VMEM((NZ, 2 * TOK, HD), bf16),
            pltpu.VMEM((NZ, 2 * TOK, HD), bf16),
            pltpu.VMEM((HD, QW), f32),
            pltpu.VMEM((1, QW), f32),
            pltpu.VMEM((1, QW), f32),
        ],
        flops=3 * 10**9,
        name="forward",
    )
    held = [stats] + [over_y(stats, -t) for t in (1, 2, 3)]
    o_came = [outs[0], over_y(outs[1], 1, False), over_y(outs[2], 2, False)]

    *dqs, dkv_own, dkv_other = call(
        backward_kernel,
        [((HD, QW), bf16)] * 3 + [((NZ, 2 * TOK, HD), bf16)] * 2,
        "s" + "v" * 16,
        (sc, *qs, *dos, *kvs, *held),
        scratch=[
            pltpu.VMEM((NZ, 2 * TOK, HD), bf16),
            pltpu.VMEM((NZ, 2 * TOK, HD), bf16),
            pltpu.VMEM((VISITS, QW, HD), bf16),
            pltpu.VMEM((VISITS, QW, HD), bf16),
            pltpu.VMEM((VISITS, HD, QW), f32),
            pltpu.VMEM((VISITS, 1, QW), f32),
            pltpu.VMEM((VISITS, 1, QW), f32),
            pltpu.VMEM((2 * TOK, HD), f32),
            pltpu.VMEM((2 * TOK, HD), f32),
        ],
        flops=5 * 10**9,
        name="backward",
    )
    dkv_home = reduce_cores_and_z(dkv_own, dkv_other, "dkv")
    dq_came = [dqs[0], over_y(dqs[1], 1, False), over_y(dqs[2], 2, False)]

    (context_send,) = call(
        context_kernel,
        [((SLOTS, QW), bf16)],
        "s" + "v" * 8,
        (sc, *o_came, *held, mh),
        scratch=[pltpu.VMEM((TOK, QW), bf16)],
        name="context",
    )
    context_came = exchange_slots(context_send)

    rg, keep, inner, *sends = call(
        rows_kernel,
        [((TOK, 768), bf16), ((TOK, 512), f32), ((8, TOK), f32)] + [((TOK + 16, 512), bf16)] * 3,
        "s" + "v" * 13,
        (sc, *dkv_home, *dq_came, cos, sin, w, *hids),
        flops=4 * 10**8,
        moved=4 * 10**6,
        name="rows",
    )
    rgs = [rg] + [over_y(rg, t) for t in (1, 2, 3)]
    totals = [over_x(a, t) for t, a in zip((1, 2, 3), sends)]
    w_own, w_other = call(
        weight_kernel,
        [((NZ, 32, 768), bf16)] * 2,
        "s" + "v" * 8,
        (sc, *ns, *rgs),
        scratch=[
            pltpu.VMEM((NY * TOK, 512), bf16),
            pltpu.VMEM((NY * TOK, 768), bf16),
            pltpu.VMEM((512, 768), f32),
        ],
        flops=4 * 10**8,
        name="weight",
    )
    w_home = reduce_cores_and_z(w_own, w_other, "weight")
    (input_grad,) = call(
        input_kernel,
        [((TOK, 512), f32)],
        "v" * 7,
        (keep, inner, *totals, inv, hidden),
        name="input",
    )
    (context,) = call(place_kernel, [((TOK, QW), bf16)], "vv", (mo, context_came), name="place")
    (weight_grad,) = call(sum_kernel, [((32, 768), f32)], "vvv", w_home, name="sum_weight")
    return context, input_grad, weight_grad


def solution(mesh):
    placed = (P("ctx", "fsdp"), P(None, "fsdp"), P(), P(), P("ctx", "fsdp"))
    return jax.shard_map(
        shards,
        mesh=mesh,
        in_specs=placed,
        out_specs=(P("ctx", "fsdp"), P("ctx", "fsdp"), P("ctx", "fsdp")),
        check_vma=False,
    )
```

```python
import functools

import jax
import jax.numpy as jnp
from jax import lax
from jax.experimental import pallas as pl
from jax.experimental.pallas import tpu as pltpu
from jax.sharding import PartitionSpec as P

HD = 128
GROUP = 4
TOK = 128
NY, NZ, NC = 4, 8, 2
N_CTX = NY * NZ * NC
NX = 4
CAP = 4
SLOTS = N_CTX * CAP
VISITS = 3
KEPT = (0, 3, 5)
FROM_BELOW = (1, 4, 6)
FROM_ABOVE = (7, 2)
QW = GROUP * TOK
epsilon = 1e-05
rope_base = 500000.0
scale = HD ** (-0.5)
log2e = 1.4426950408889634
masked = -1e30

f32, bf16, i32 = jnp.float32, jnp.bfloat16, jnp.int32

NT = (((1,), (1,)), ((), ()))
NN = (((1,), (0,)), ((), ()))
TN = (((0,), (0,)), ((), ()))


def dot(a, b, dims=NN):
    return lax.dot_general(a, b, dims, preferred_element_type=f32)


def call(kernel, outs, in_kinds, args, scratch=(), flops=10**8, moved=2 * 10**6, name=None, out_kinds=None):
    vm = pl.BlockSpec(memory_space=pltpu.VMEM)
    sm = pl.BlockSpec(memory_space=pltpu.SMEM)
    hbm = pl.BlockSpec(memory_space=pltpu.HBM)
    anywhere = pl.BlockSpec(memory_space=pl.ANY)
    return pl.pallas_call(
        kernel,
        out_shape=[jax.ShapeDtypeStruct(s, d) for s, d in outs],
        in_specs=[{"s": sm, "v": vm, "h": hbm, "a": anywhere}[k] for k in in_kinds],
        out_specs=[{"v": vm, "h": hbm}[k] for k in out_kinds or "v" * len(outs)],
        scratch_shapes=list(scratch),
        compiler_params=pltpu.CompilerParams(vmem_limit_bytes=16 * 1024 * 1024),
        cost_estimate=pl.CostEstimate(flops=1000, bytes_accessed=1000, transcendentals=0),
        name=name,
    )(*args)


def scalars(lengths):
    me = lax.axis_index("ctx").astype(i32)
    x = lax.axis_index("fsdp").astype(i32)
    return [me, me // (NZ * NC), me // NC % NZ, me % NC, x, None, None, None] + [lengths[d] for d in range(8)]


def one_hot(condition):
    return jnp.where(condition, 1.0, 0.0).astype(bf16)


def route_kernel(lengths, owners, cg, send_ref, mh_ref, from_owners_ref, from_homes_ref):
    sc = scalars(lengths)
    me, core = sc[0], sc[3]
    mine = one_hot(owners[...] == me)
    count = dot(mine, jnp.ones((TOK, TOK), bf16)).astype(bf16)
    slot = lax.broadcasted_iota(i32, (SLOTS, TOK), 0)
    place = lax.broadcasted_iota(i32, (SLOTS, TOK), 1).astype(f32)
    rank = (slot % CAP).astype(f32)
    source = lax.broadcasted_iota(i32, (SLOTS, N_CTX), 1)
    slot_row = lax.broadcasted_iota(i32, (SLOTS, N_CTX), 0)

    def owned(home):
        base = dot(one_hot(source < home), count)
        here = dot(one_hot(source == home), count)
        return (base + rank == place) & (rank < here)

    send_ref[...] = dot(one_hot(owned(slot_row // CAP)), cg[...]).astype(bf16)
    for_me = slot // CAP % NC == core
    for e in range(NC):
        sender = slot_row // (NC * CAP) * NC + (core ^ e)
        from_homes_ref[e * SLOTS : (e + 1) * SLOTS, :] = one_hot(owned(sender) & for_me)

    own = jnp.broadcast_to(owners[pl.ds(me, 1), :].astype(f32), (TOK, TOK))
    earlier = lax.broadcasted_iota(i32, (TOK, TOK), 0) < lax.broadcasted_iota(i32, (TOK, TOK), 1)
    same = jnp.where((own == own.T) & earlier, 1.0, 0.0)
    own_rank = jnp.sum(same, axis=0, keepdims=True).astype(i32)
    owner = own[0:1, :].astype(i32)
    mh_ref[...] = one_hot(slot == owner * CAP + own_rank)
    came_slot = owner // NC * (NC * CAP) + core * CAP + own_rank
    for e in range(NC):
        here = (slot == came_slot) & (owner % NC == (core ^ e))
        from_owners_ref[e * SLOTS : (e + 1) * SLOTS, :] = one_hot(here)


def place_rows(matrix, same_core, other_core):
    rows = dot(matrix[0:SLOTS, :], same_core[...], TN) + dot(matrix[SLOTS:, :], other_core[...], TN)
    return rows.astype(bf16)


def grad_home_kernel(matrix, same_core, other_core, out_ref):
    rows = place_rows(matrix, same_core, other_core)
    for h in range(GROUP):
        out_ref[h * TOK : (h + 1) * TOK, :] = rows[:, h * HD : (h + 1) * HD]


def place_kernel(matrix, same_core, other_core, out_ref):
    out_ref[...] = place_rows(matrix, same_core, other_core)


def turn(t, c, s):
    return t * c + pltpu.roll(t, HD // 2, 1) * s


def turn_back(t, c, s):
    return t * c - pltpu.roll(t, HD // 2, 1) * s


def project_kernel(lengths, *refs):
    sc = scalars(lengths)
    hids, (w, cos, sin) = refs[0:4], refs[4:7]
    q_ref, kv_ref, *ns, inv_ref, held, out_sems = refs[7:]
    y, x = sc[1], sc[4]
    blocks = [h[...].astype(f32) for h in hids]
    square = sum(jnp.sum(b * b, axis=1, keepdims=True) for b in blocks)
    inv = lax.rsqrt(square * (1.0 / (NX * 512)) + epsilon)
    inv_ref[...] = jnp.broadcast_to(inv, (TOK, HD))
    for s in range(NX):
        held[(x + NX - s) % NX] = (blocks[s] * inv).astype(bf16)
    out_copies = [
        pltpu.make_async_copy(held.at[(y + t) % NX], out, out_sems.at[t]) for t, out in enumerate(ns)
    ]
    for copy in out_copies:
        copy.start()
    total = jnp.zeros((TOK, 768), f32)
    for k in range(NX):
        total = total + dot(held[k], w[k * 512 : (k + 1) * 512, :])
    c, s = cos[...], sin[...]
    for h in range(GROUP):
        q_ref[h * TOK : (h + 1) * TOK, :] = turn(total[:, h * HD : (h + 1) * HD], c, s).astype(bf16)
    kv_ref[0:TOK, :] = turn(total[:, 512:640], c, s).astype(bf16)
    kv_ref[TOK:, :] = total[:, 640:768].astype(bf16)
    for copy in out_copies:
        copy.wait()


def block_start(sc, row):
    start, begin = 0, sc[8]
    for d in range(1, 8):
        start = jnp.where(begin <= row, begin, start)
        begin = begin + sc[8 + d]
    return start


def query_rows(sc, visit):
    first = ((sc[1] + visit) * NZ * NC + sc[2] * NC + sc[3]) * TOK
    rows = first + lax.broadcasted_iota(i32, (1, QW), 1) % TOK
    starts, begin = jnp.zeros((1, QW), i32), sc[8]
    for d in range(1, 8):
        starts = jnp.where(rows >= begin, begin, starts)
        begin = begin + sc[8 + d]
    return first, rows, starts


def key_tile(sc, s):
    return sc[1] * NZ + (sc[2] + NZ - s) % NZ


def tile_needed(sc, visit, s):
    pair = key_tile(sc, s)
    first = ((sc[1] + visit) * NZ * NC + sc[2] * NC + sc[3]) * TOK
    live = (sc[1] + visit < NY) & (pair <= (sc[1] + visit) * NZ + sc[2])
    return live & (pair * 256 + 255 >= block_start(sc, first))


def load_keys(kvs, keys, values):
    for e in range(NC):
        for stack, steps in zip(kvs[3 * e : 3 * e + 3], (KEPT, FROM_BELOW, FROM_ABOVE)):
            for i, s in enumerate(steps):
                keys[s, e * TOK : (e + 1) * TOK, :] = stack[i, 0:TOK, :]
                values[s, e * TOK : (e + 1) * TOK, :] = stack[i, TOK:, :]


def pack_kernel(b0, b3, b5, _, __, three_ref, two_ref):
    for i, b in enumerate((b0, b3, b5)):
        three_ref[i] = b[...]
        if i < 2:
            two_ref[i] = b[...]


def tile_mask(sc, s, rows, starts):
    offset = lax.broadcasted_iota(i32, (2 * TOK, QW), 0) ^ (sc[3] * TOK)
    key_rows = key_tile(sc, s) * 256 + offset
    return (key_rows >= starts) & (key_rows <= rows)


def forward_kernel(lengths, *refs):
    sc = scalars(lengths)
    qs, kvs = refs[0:3], refs[3:9]
    outs, stats = refs[9:12], refs[12]
    keys, values, acc, top, total = refs[13:]
    load_keys(kvs, keys, values)
    stats[...] = jnp.zeros_like(stats)
    for visit in range(VISITS):
        q_ref = qs[visit]
        _, rows, starts = query_rows(sc, visit)
        acc[...] = jnp.zeros_like(acc)
        total[...] = jnp.zeros_like(total)
        top[...] = jnp.full_like(top, masked)

        @pl.loop(0, NZ)
        def _(s):
            @pl.when(tile_needed(sc, visit, s))
            def _():
                scores = dot(keys[s], q_ref[...], NT) * (scale * log2e)
                scores = jnp.where(tile_mask(sc, s, rows, starts), scores, masked)
                old = top[...]
                new = jnp.maximum(old, jnp.max(scores, axis=0, keepdims=True))
                base = jnp.maximum(new, 0.1 * masked)
                p = jnp.exp2(scores - base)
                fade = jnp.exp2(old - base)
                top[...] = new
                total[...] = total[...] * fade + jnp.sum(p, axis=0, keepdims=True)
                acc[...] = acc[...] * fade + dot(values[s], p.astype(bf16), TN)

        mass = total[...]
        some = mass > 0.0
        mass = jnp.where(some, mass, 1.0)
        outs[visit][...] = (acc[...] * (1.0 / mass)).astype(bf16)
        stats[visit : visit + 1, :] = jnp.where(some, top[...] + jnp.log2(mass), masked)


def delta_kernel(stats, o0, o1, o2, d0, d1, d2, out_ref):
    out_ref[0:4, :] = stats[0:4, :]
    for visit, (o, d) in enumerate(((o0, d0), (o1, d1), (o2, d2))):
        product = d[...].astype(f32).T * o[...].astype(f32)
        out_ref[4 + visit : 5 + visit, :] = jnp.sum(product, axis=0, keepdims=True)
    out_ref[7:8, :] = jnp.zeros((1, QW), f32)


def combine_stats(sc, visit, held):
    logs, deltas = [], []
    for j in range(VISITS):
        t = visit - j
        logs.append(jnp.where(sc[1] + t >= 0, held[t % NY][j : j + 1, :], masked))
        deltas.append(held[t % NY][4 + j : 5 + j, :])
    top = functools.reduce(jnp.maximum, logs)
    weights = [jnp.exp2(v - top) for v in logs]
    mass = sum(weights)
    weights = [v / mass for v in weights]
    return top + jnp.log2(mass), sum(a * b for a, b in zip(weights, deltas)), weights


def backward_kernel(lengths, *refs):
    sc = scalars(lengths)
    qs, dos, kvs, held, outs = refs[0:3], refs[3:6], refs[6:12], refs[12:16], refs[16:18]
    dq_ref, returns, own_ref, other_ref = refs[18], refs[19:21], refs[21], refs[22]
    keys, values, q_all, do_all, dq_acc, logs, deltas, dk, dv = refs[23:]
    load_keys(kvs, keys, values)
    dq_acc[...] = jnp.zeros_like(dq_acc)
    for visit in range(VISITS):
        q_all[visit] = qs[visit][...]
        do_all[visit] = dos[visit][...]
        log_total, delta, _ = combine_stats(sc, visit, held)
        logs[visit] = log_total
        deltas[visit] = delta

    @pl.loop(0, NZ)
    def _(s):
        dk[...] = jnp.zeros_like(dk)
        dv[...] = jnp.zeros_like(dv)

        @pl.loop(0, VISITS)
        def _(visit):
            @pl.when(tile_needed(sc, visit, s))
            def _():
                _, rows, starts = query_rows(sc, visit)
                q, do = q_all[visit], do_all[visit]
                scores = dot(keys[s], q, NT) * (scale * log2e) - logs[visit]
                p = jnp.exp2(jnp.where(tile_mask(sc, s, rows, starts), scores, masked))
                dp = dot(values[s], do, NT)
                ds = (p * (dp - deltas[visit])).astype(bf16)
                dv[...] += dot(p.astype(bf16), do)
                dk[...] += dot(ds, q)
                dq_acc[visit] += dot(keys[s], ds, TN)

        for e, out in enumerate((own_ref, other_ref)):
            half = slice(e * TOK, (e + 1) * TOK)
            out[s, 0:TOK, :] = (dk[half, :] * scale).astype(bf16)
            out[s, TOK:, :] = dv[half, :].astype(bf16)

    dq_ref[...] = dq_acc[0] * scale
    for visit in (1, 2):
        returns[visit - 1][0:HD, :] = outs[visit - 1][...]
        returns[visit - 1][HD:, :] = (dq_acc[visit] * scale).astype(bf16)


def context_kernel(lengths, o0, o1, o2, s0, s1, s2, s3, mh, _, send_ref, rows):
    sc = scalars(lengths)
    _, _, weights = combine_stats(sc, 0, (s0, s1, s2, s3))
    out = o0[...].astype(f32) * weights[0]
    for j, o in ((1, o1), (2, o2)):
        out = out + jnp.where(sc[1] >= j, o[0:HD, :].astype(f32), 0.0) * weights[j]
    for h in range(GROUP):
        rows[:, h * HD : (h + 1) * HD] = out[:, h * TOK : (h + 1) * TOK].T.astype(bf16)
    send_ref[...] = dot(mh[...], rows[...]).astype(bf16)


def add_cores_kernel(own, came, kept, below, above):
    for out, steps in ((kept, KEPT), (below, FROM_BELOW), (above, FROM_ABOVE)):
        for i, s in enumerate(steps):
            out[i] = (own[s].astype(f32) + came[s].astype(f32)).astype(out.dtype)


def add_near_kernel(kept, below, above, *refs):
    o0, o3, o5 = refs[-3:]
    o0[...] = kept[0] + below[0].astype(f32) + above[0].astype(f32)
    o3[...] = (kept[1] + below[1].astype(f32) + above[1].astype(f32)).astype(bf16)
    o5[...] = (kept[2] + below[2].astype(f32)).astype(bf16)


def rows_kernel(lengths, *refs):
    sc = scalars(lengths)
    parts, dqs, (cos, sin, rg_ref) = refs[0:3], refs[3:6], refs[6:9]
    c, s = cos[...], sin[...]
    dq = dqs[0][...]
    for j in (1, 2):
        dq = dq + jnp.where(sc[1] >= j, dqs[j][HD:, :].astype(f32), 0.0)
    for h in range(GROUP):
        rg_ref[:, h * HD : (h + 1) * HD] = turn_back(dq[:, h * TOK : (h + 1) * TOK].T, c, s).astype(bf16)
    dkv = sum(p[...].astype(f32) for p in parts)
    rg_ref[:, 512:640] = turn_back(dkv[0:TOK], c, s).astype(bf16)
    rg_ref[:, 640:768] = dkv[TOK:].astype(bf16)


def spread_kernel(lengths, *refs):
    sc = scalars(lengths)
    rg_ref, w, hids = refs[0], refs[1], refs[2:6]
    keep_ref, inner_ref, sends = refs[9], refs[10], refs[11:14]
    kept, sem = refs[14:]
    x = sc[4]
    rg = rg_ref[...]
    inner = jnp.zeros((TOK, 1), f32)
    for t in range(NX):
        first = pl.multiple_of((x + t) % NX * 512, 512)
        part = dot(rg, w[pl.ds(first, 512), :], NT)
        inner = inner + jnp.sum(part * hids[-t % NX][...].astype(f32), axis=1, keepdims=True)
        if t == 0:
            kept[...] = part
            keep_copy = pltpu.make_async_copy(kept, keep_ref, sem)
            keep_copy.start()
        else:
            sends[t - 1][0:TOK, :] = part.astype(bf16)
    row = jnp.broadcast_to(inner, (TOK, TOK)).T[0:16, :]
    inner_ref[...] = row[0:8, :]
    high = row.astype(bf16).astype(f32)
    line = lax.broadcasted_iota(i32, (16, TOK), 0)
    both = jnp.where(line == 0, high, jnp.where(line == 1, row - high, 0.0)).astype(bf16)
    for out in sends:
        out[TOK:, :] = jnp.concatenate([both, jnp.zeros((16, 384), bf16)], axis=1)
    keep_copy.wait()


def input_kernel(keep, inner, r1, r2, r3, inv_ref, hid, out_ref):
    total = keep[...]
    row = inner[0:1, :]
    for r in (r1, r2, r3):
        total = total + r[0:TOK, :].astype(f32)
        tail = r[TOK:, 0:TOK].astype(f32)
        row = row + tail[0:1, :] + tail[1:2, :]
    column = jnp.broadcast_to(row, (TOK, TOK)).T[:, 0:1]
    inv = inv_ref[:, 0:1]
    out_ref[...] = inv * total - hid[...].astype(f32) * (inv * inv * inv * column * (1.0 / (NX * 512)))


def weight_kernel(lengths, *refs):
    sc = scalars(lengths)
    ns, rgs, own_ref, other_ref = refs[0:4], refs[4:8], refs[8], refs[9]
    n_all, rg_all, product, sems = refs[10:]
    copies = [pltpu.make_async_copy(ns[t], n_all.at[pl.ds(t * TOK, TOK), :], sems.at[t]) for t in range(NY)]
    for copy in copies:
        copy.start()
    for t in range(NY):
        rg_all[t * TOK : (t + 1) * TOK, :] = rgs[t][...]
    for copy in copies:
        copy.wait()
    product[...] = dot(n_all[...], rg_all[...], TN)
    z, core = sc[2], sc[3]
    for s in range(NZ):
        first = ((z + NZ - s) % NZ) * 64
        own_ref[s] = product[pl.ds(pl.multiple_of(first + core * 32, 32), 32), :].astype(bf16)
        other_ref[s] = product[pl.ds(pl.multiple_of(first + (1 - core) * 32, 32), 32), :].astype(bf16)


def sum_kernel(*refs):
    refs[-1][...] = sum(r[...].astype(f32) for r in refs[:-1])


def index_of(y, z, c):
    return (y * NZ + z) * NC + c


def over_y(a, shift, wrap=True):
    pairs = [
        (index_of(y, z, c), index_of((y + shift) % NY, z, c))
        for y in range(NY)
        for z in range(NZ)
        for c in range(NC)
        if wrap or 0 <= y + shift < NY
    ]
    return lax.ppermute(a, "ctx", pairs)


def over_z(a, shift):
    pairs = [
        (index_of(y, z, c), index_of(y, (z + shift) % NZ, c))
        for y in range(NY)
        for z in range(NZ)
        for c in range(NC)
    ]
    return lax.ppermute(a, "ctx", pairs)


def over_c(a):
    pairs = [(index_of(y, z, c), index_of(y, z, 1 - c)) for y in range(NY) for z in range(NZ) for c in range(NC)]
    return lax.ppermute(a, "ctx", pairs)


def over_x(a, shift):
    return lax.ppermute(a, "fsdp", [(x, (x + shift) % NX) for x in range(NX)])


def exchange_slots(send):
    width = send.shape[1]
    groups = [[index_of(y, z, c) for y in range(NY) for z in range(NZ)] for c in range(NC)]
    came = lax.all_to_all(
        send.reshape(NY * NZ, NC * CAP, width), "ctx", split_axis=0, concat_axis=0, tiled=True, axis_index_groups=groups
    )
    return came.reshape(SLOTS, width)


def reduce_cores_and_z(own, other, name, after=()):
    shape = own.shape[1:]
    came = over_c(other)
    kept, below, above = call(
        add_cores_kernel,
        [((3,) + shape, f32), ((3,) + shape, bf16), ((2,) + shape, bf16)],
        "vv",
        (own, came),
        name="add_cores_" + name,
    )
    below, above = over_z(below, -1), over_z(above, 1)
    o0, o3, o5 = call(
        add_near_kernel,
        [(shape, f32), (shape, bf16), (shape, bf16)],
        "vvv" + "a" * len(after),
        (kept, below, above, *after),
        name="add_near_" + name,
    )
    return o0, over_z(o3, -3), over_z(o5, 3)


def shards(hidden, w, doc_lengths, owners, context_grad):
    lengths = doc_lengths.astype(i32)
    hids = [hidden] + [over_x(hidden, s) for s in range(1, NX)]

    grad_send, mh, from_owners, from_homes = call(
        route_kernel,
        [((SLOTS, QW), bf16), ((SLOTS, TOK), bf16), ((NC * SLOTS, TOK), bf16), ((NC * SLOTS, TOK), bf16)],
        "svv",
        (lengths, owners.reshape(N_CTX, TOK), context_grad),
        name="route",
    )
    arrived = exchange_slots(grad_send)

    home = lax.axis_index("ctx").astype(i32) * TOK + jnp.arange(TOK, dtype=i32)
    docs = jnp.arange(8, dtype=i32)
    doc_starts = jnp.sum(jnp.where(docs[:, None] > docs[None, :], lengths[None, :], 0), axis=1)
    start = jnp.max(jnp.where(home[:, None] >= doc_starts[None, :], doc_starts[None, :], 0), axis=1)
    frequency = rope_base ** (-(2.0 * jnp.arange(HD // 2, dtype=f32)) / HD)
    angles = (home - start).astype(f32)[:, None] * frequency[None, :]
    cos, sin = jnp.cos(angles), jnp.sin(angles)
    cos, sin = jnp.concatenate([cos, cos], axis=1), jnp.concatenate([-sin, sin], axis=1)

    q, kv, n0, n1, n2, n3, inv = call(
        project_kernel,
        [((QW, HD), bf16), ((2 * TOK, HD), bf16)] + [((TOK, 512), bf16)] * 4 + [((TOK, HD), f32)],
        "svvvvvvv",
        (lengths, *hids, w, cos, sin),
        scratch=[pltpu.VMEM((NX, TOK, 512), bf16), pltpu.SemaphoreType.DMA((NX,))],
        out_kinds="vvhhhhv",
        flops=4 * 10**8,
        moved=4 * 10**6,
        name="project",
    )
    qs = [q, over_y(q, -1, False), over_y(q, -2, False)]
    three, two = call(
        pack_kernel,
        [((3, 2 * TOK, HD), bf16), ((2, 2 * TOK, HD), bf16)],
        "vvvaa",
        (kv, over_z(kv, 3), over_z(kv, -3), qs[1], qs[2]),
        name="pack",
    )
    kv_own = [three, over_z(three, 1), over_z(two, -1)]
    kvs = kv_own + [over_c(a) for a in kv_own]
    ns = [n0] + [over_y(n, t) for t, n in ((1, n1), (2, n2), (3, n3))]

    (do,) = call(
        grad_home_kernel, [((QW, HD), bf16)], "vvv", (from_owners, arrived, over_c(arrived)), name="grad_home"
    )
    dos = [do, over_y(do, -1, False), over_y(do, -2, False)]

    *outs, stats = call(
        forward_kernel,
        [((HD, QW), bf16)] * 3 + [((8, QW), f32)],
        "s" + "v" * 9,
        (lengths, *qs, *kvs),
        scratch=[
            pltpu.VMEM((NZ, 2 * TOK, HD), bf16),
            pltpu.VMEM((NZ, 2 * TOK, HD), bf16),
            pltpu.VMEM((HD, QW), f32),
            pltpu.VMEM((1, QW), f32),
            pltpu.VMEM((1, QW), f32),
        ],
        flops=3 * 10**9,
        name="forward",
    )
    (stats,) = call(delta_kernel, [((8, QW), f32)], "v" * 7, (stats, *outs, *dos), name="delta")
    held = [stats] + [over_y(stats, -t) for t in (1, 2, 3)]

    dq, back1, back2, dkv_own, dkv_other = call(
        backward_kernel,
        [((HD, QW), f32)] + [((2 * HD, QW), bf16)] * 2 + [((NZ, 2 * TOK, HD), bf16)] * 2,
        "s" + "v" * 18,
        (lengths, *qs, *dos, *kvs, *held, outs[1], outs[2]),
        scratch=[
            pltpu.VMEM((NZ, 2 * TOK, HD), bf16),
            pltpu.VMEM((NZ, 2 * TOK, HD), bf16),
            pltpu.VMEM((VISITS, QW, HD), bf16),
            pltpu.VMEM((VISITS, QW, HD), bf16),
            pltpu.VMEM((VISITS, HD, QW), f32),
            pltpu.VMEM((VISITS, 1, QW), f32),
            pltpu.VMEM((VISITS, 1, QW), f32),
            pltpu.VMEM((2 * TOK, HD), f32),
            pltpu.VMEM((2 * TOK, HD), f32),
        ],
        flops=5 * 10**9,
        name="backward",
    )
    back1, back2 = over_y(back1, 1, False), over_y(back2, 2, False)

    dkv_home = reduce_cores_and_z(dkv_own, dkv_other, "dkv")
    (rg,) = call(
        rows_kernel,
        [((TOK, 768), bf16)],
        "s" + "v" * 8,
        (lengths, *dkv_home, dq, back1, back2, cos, sin),
        name="rows",
    )
    rgs = [rg] + [over_y(rg, t) for t in (1, 2, 3)]
    keep, inner, *sends = call(
        spread_kernel,
        [((TOK, 512), f32), ((8, TOK), f32)] + [((TOK + 16, 512), bf16)] * 3,
        "svvvvvvaaa",
        (lengths, rg, w, *hids, *ns[1:]),
        scratch=[pltpu.VMEM((TOK, 512), f32), pltpu.SemaphoreType.DMA],
        name="spread",
        out_kinds="hvvvv",
    )
    (context_send,) = call(
        context_kernel,
        [((SLOTS, QW), bf16)],
        "s" + "v" * 8 + "a",
        (lengths, outs[0], back1, back2, *held, mh, inner),
        scratch=[pltpu.VMEM((TOK, QW), bf16)],
        name="context",
    )
    context_came = exchange_slots(context_send)

    totals = [over_x(a, t) for t, a in zip((1, 2, 3), sends)]
    w_own, w_other = call(
        weight_kernel,
        [((NZ, 32, 768), bf16)] * 2,
        "s" + "h" * 4 + "v" * 4,
        (lengths, *ns, *rgs),
        scratch=[
            pltpu.VMEM((NY * TOK, 512), bf16),
            pltpu.VMEM((NY * TOK, 768), bf16),
            pltpu.VMEM((512, 768), f32),
            pltpu.SemaphoreType.DMA((NY,)),
        ],
        flops=4 * 10**8,
        name="weight",
    )
    w_home = reduce_cores_and_z(w_own, w_other, "weight")
    (input_grad,) = call(
        input_kernel,
        [((TOK, 512), f32)],
        "v" * 7,
        (keep, inner, *totals, inv, hidden),
        name="input",
    )
    (context,) = call(
        place_kernel, [((TOK, QW), bf16)], "vvv", (from_homes, context_came, over_c(context_came)), name="place"
    )
    (weight_grad,) = call(sum_kernel, [((32, 768), f32)], "vvv", w_home, name="sum_weight")
    return context, input_grad, weight_grad


def solution(mesh):
    placed = (P("ctx", "fsdp"), P(None, "fsdp"), P(), P(), P("ctx", "fsdp"))
    return jax.shard_map(
        shards,
        mesh=mesh,
        in_specs=placed,
        out_specs=(P("ctx", "fsdp"), P("ctx", "fsdp"), P("ctx", "fsdp")),
        check_vma=False,
    )
```

```python
import functools

import jax
import jax.numpy as jnp
from jax import lax
from jax.experimental import pallas as pl
from jax.experimental.pallas import tpu as pltpu
from jax.sharding import PartitionSpec as P

HD = 128
GROUP = 4
TOK = 128
NY, NZ, NC = 4, 8, 2
N_CTX = NY * NZ * NC
NX = 4
CAP = 4
SLOTS = N_CTX * CAP
VISITS = 3
TILE = 512
KEPT = (0, 3, 5)
FROM_BELOW = (1, 4, 6)
FROM_ABOVE = (7, 2)
QW = GROUP * TOK
epsilon = 1e-05
rope_base = 500000.0
scale = HD ** (-0.5)
log2e = 1.4426950408889634
masked = -1e30

f32, bf16, i32 = jnp.float32, jnp.bfloat16, jnp.int32

NT = (((1,), (1,)), ((), ()))
NN = (((1,), (0,)), ((), ()))
TN = (((0,), (0,)), ((), ()))


def dot(a, b, dims=NN):
    return lax.dot_general(a, b, dims, preferred_element_type=f32)


def call(kernel, outs, in_kinds, args, scratch=(), flops=10**8, moved=2 * 10**6, name=None, out_kinds=None):
    vm = pl.BlockSpec(memory_space=pltpu.VMEM)
    sm = pl.BlockSpec(memory_space=pltpu.SMEM)
    hbm = pl.BlockSpec(memory_space=pltpu.HBM)
    anywhere = pl.BlockSpec(memory_space=pl.ANY)
    return pl.pallas_call(
        kernel,
        out_shape=[jax.ShapeDtypeStruct(s, d) for s, d in outs],
        in_specs=[{"s": sm, "v": vm, "h": hbm, "a": anywhere}[k] for k in in_kinds],
        out_specs=[{"v": vm, "h": hbm}[k] for k in out_kinds or "v" * len(outs)],
        scratch_shapes=list(scratch),
        compiler_params=pltpu.CompilerParams(vmem_limit_bytes=16 * 1024 * 1024),
        cost_estimate=pl.CostEstimate(flops=1000, bytes_accessed=1000, transcendentals=0),
        name=name,
    )(*args)


def scalars(lengths):
    me = lax.axis_index("ctx").astype(i32)
    x = lax.axis_index("fsdp").astype(i32)
    return [me, me // (NZ * NC), me // NC % NZ, me % NC, x, None, None, None] + [lengths[d] for d in range(8)]


def one_hot(condition):
    return jnp.where(condition, 1.0, 0.0).astype(bf16)


def route_kernel(lengths, owners, cg, send_ref, mh_ref, from_owners_ref, from_homes_ref):
    sc = scalars(lengths)
    me, core = sc[0], sc[3]
    mine = one_hot(owners[...] == me)
    count = dot(mine, jnp.ones((TOK, TOK), bf16)).astype(bf16)
    slot = lax.broadcasted_iota(i32, (SLOTS, TOK), 0)
    place = lax.broadcasted_iota(i32, (SLOTS, TOK), 1).astype(f32)
    rank = (slot % CAP).astype(f32)
    source = lax.broadcasted_iota(i32, (SLOTS, N_CTX), 1)
    slot_row = lax.broadcasted_iota(i32, (SLOTS, N_CTX), 0)

    def owned(home):
        base = dot(one_hot(source < home), count)
        here = dot(one_hot(source == home), count)
        return (base + rank == place) & (rank < here)

    send_ref[...] = dot(one_hot(owned(slot_row // CAP)), cg[...]).astype(bf16)
    for_me = slot // CAP % NC == core
    for e in range(NC):
        sender = slot_row // (NC * CAP) * NC + (core ^ e)
        from_homes_ref[e * SLOTS : (e + 1) * SLOTS, :] = one_hot(owned(sender) & for_me)

    own = jnp.broadcast_to(owners[pl.ds(me, 1), :].astype(f32), (TOK, TOK))
    earlier = lax.broadcasted_iota(i32, (TOK, TOK), 0) < lax.broadcasted_iota(i32, (TOK, TOK), 1)
    same = jnp.where((own == own.T) & earlier, 1.0, 0.0)
    own_rank = jnp.sum(same, axis=0, keepdims=True).astype(i32)
    owner = own[0:1, :].astype(i32)
    mh_ref[...] = one_hot(slot == owner * CAP + own_rank)
    came_slot = owner // NC * (NC * CAP) + core * CAP + own_rank
    for e in range(NC):
        here = (slot == came_slot) & (owner % NC == (core ^ e))
        from_owners_ref[e * SLOTS : (e + 1) * SLOTS, :] = one_hot(here)


def place_rows(matrix, same_core, other_core):
    rows = dot(matrix[0:SLOTS, :], same_core[...], TN) + dot(matrix[SLOTS:, :], other_core[...], TN)
    return rows.astype(bf16)


def grad_home_kernel(matrix, same_core, other_core, out_ref):
    rows = place_rows(matrix, same_core, other_core)
    for h in range(GROUP):
        out_ref[h * TOK : (h + 1) * TOK, :] = rows[:, h * HD : (h + 1) * HD]


def place_kernel(matrix, same_core, other_core, out_ref):
    out_ref[...] = place_rows(matrix, same_core, other_core)


def turn(t, c, s):
    return t * c + pltpu.roll(t, HD // 2, 1) * s


def turn_back(t, c, s):
    return t * c - pltpu.roll(t, HD // 2, 1) * s


def project_kernel(lengths, *refs):
    sc = scalars(lengths)
    hids, (w, cos, sin) = refs[0:4], refs[4:7]
    q_ref, kv_ref, *ns, inv_ref, held, out_sems = refs[7:]
    y, x = sc[1], sc[4]
    blocks = [h[...].astype(f32) for h in hids]
    square = sum(jnp.sum(b * b, axis=1, keepdims=True) for b in blocks)
    inv = lax.rsqrt(square * (1.0 / (NX * 512)) + epsilon)
    inv_ref[...] = jnp.broadcast_to(inv, (TOK, HD))
    for s in range(NX):
        held[(x + NX - s) % NX] = (blocks[s] * inv).astype(bf16)
    out_copies = [
        pltpu.make_async_copy(held.at[(y + t) % NX], out, out_sems.at[t]) for t, out in enumerate(ns)
    ]
    for copy in out_copies:
        copy.start()
    total = jnp.zeros((TOK, 768), f32)
    for k in range(NX):
        total = total + dot(held[k], w[k * 512 : (k + 1) * 512, :])
    c, s = cos[...], sin[...]
    for h in range(GROUP):
        q_ref[h * TOK : (h + 1) * TOK, :] = turn(total[:, h * HD : (h + 1) * HD], c, s).astype(bf16)
    kv_ref[0:TOK, :] = turn(total[:, 512:640], c, s).astype(bf16)
    kv_ref[TOK:, :] = total[:, 640:768].astype(bf16)
    for copy in out_copies:
        copy.wait()


def turn_heads(rows, out):
    for h in range(GROUP):
        part = slice(h * TOK, (h + 1) * TOK)
        out[:, part] = rows[part, :].astype(f32).T.astype(bf16)


def doc_start(sc, row):
    start, begin = 0, sc[8]
    for d in range(1, 8):
        start = jnp.where(begin <= row, begin, start)
        begin = begin + sc[8 + d]
    return start


def first_query(sc, visit):
    return ((sc[1] + visit) * NZ * NC + sc[2] * NC + sc[3]) * TOK


def key_tile(sc, s):
    return sc[1] * NZ + (sc[2] + NZ - s) % NZ


def tile_state(sc, visit, s):
    first, low = first_query(sc, visit), key_tile(sc, s) * (NC * TOK)
    high = low + NC * TOK - 1
    some = (sc[1] + visit < NY) & (low <= first + TOK - 1) & (high >= doc_start(sc, first))
    every = (high <= first) & (low >= doc_start(sc, first + TOK - 1))
    return some, every


def tile_mask(sc, visit, s):
    rows = first_query(sc, visit) + lax.broadcasted_iota(i32, (1, TOK), 1)
    starts = doc_start(sc, rows)
    line = lax.broadcasted_iota(i32, (TILE, TOK), 0)
    offset = (line % (NC * TOK)) ^ (sc[3] * TOK)
    first, second = key_tile(sc, 2 * s) * (NC * TOK), key_tile(sc, 2 * s + 1) * (NC * TOK)
    key_rows = jnp.where(line < NC * TOK, first, second) + offset
    return (key_rows >= starts) & (key_rows <= rows)


def on_tile(sc, visit, s, work):
    some, every = tile_state(sc, visit, 2 * s)
    some2, every2 = tile_state(sc, visit, 2 * s + 1)
    some, every = some | some2, every & every2

    @pl.when(some & every)
    def _():
        work(None)

    @pl.when(some & jnp.logical_not(every))
    def _():
        work(tile_mask(sc, visit, s))


def load_keys(kvs, keys, values, turned, which):
    for e in range(NC):
        for stack, steps in zip(kvs[3 * e : 3 * e + 3], (KEPT, FROM_BELOW, FROM_ABOVE)):
            for i, s in enumerate(steps):
                at = s // 2
                half = slice((s % 2 * NC + e) * TOK, (s % 2 * NC + e + 1) * TOK)
                keys[at, half, :] = stack[i, 0:TOK, :]
                values[at, half, :] = stack[i, TOK:, :]
                picked = stack[i, which * TOK : (which + 1) * TOK, :]
                turned[at, :, half] = picked.astype(f32).T.astype(bf16)


def pack_kernel(b0, b3, b5, _, __, three_ref, two_ref):
    for i, b in enumerate((b0, b3, b5)):
        three_ref[i] = b[...]
        if i < 2:
            two_ref[i] = b[...]


def forward_kernel(lengths, *refs):
    sc = scalars(lengths)
    qs, kvs = refs[0:3], refs[3:9]
    outs, stats = refs[9:12], refs[12]
    keys, values, values_t, probs, acc, top, total, q_t = refs[13:]
    load_keys(kvs, keys, values, values_t, 1)
    stats[...] = jnp.zeros_like(stats)
    for visit in range(VISITS):
        turn_heads(qs[visit], q_t)
        acc[...] = jnp.zeros_like(acc)
        total[...] = jnp.zeros_like(total)
        top[...] = jnp.full_like(top, masked)

        @pl.loop(0, NZ // 2)
        def _(s):
            def work(allowed):
                for h in range(GROUP):
                    cols = slice(h * TOK, (h + 1) * TOK)
                    scores = dot(keys[s], q_t[:, cols])
                    if allowed is not None:
                        scores = jnp.where(allowed, scores, masked)
                    old = top[:, cols]
                    new = jnp.maximum(old, jnp.max(scores, axis=0, keepdims=True))
                    base = jnp.maximum(new, 0.1 * masked) * (scale * log2e)
                    p = jnp.exp2(scores * (scale * log2e) - base)
                    fade = jnp.exp2(old * (scale * log2e) - base)
                    top[:, cols] = new
                    total[:, cols] = total[:, cols] * fade + jnp.sum(p, axis=0, keepdims=True)
                    probs[:, cols] = p.astype(bf16)
                    acc[:, cols] = acc[:, cols] * fade
                acc[...] += dot(values_t[s], probs[...])

            on_tile(sc, visit, s, work)

        mass = total[...]
        some = mass > 0.0
        mass = jnp.where(some, mass, 1.0)
        outs[visit][...] = (acc[...] * (1.0 / mass)).astype(bf16)
        logs = top[...] * (scale * log2e) + jnp.log2(mass)
        stats[visit : visit + 1, :] = jnp.where(some, logs, masked)


def delta_kernel(stats, o0, o1, o2, d0, d1, d2, out_ref):
    out_ref[0:4, :] = stats[0:4, :]
    for visit, (o, d) in enumerate(((o0, d0), (o1, d1), (o2, d2))):
        product = d[...].astype(f32).T * o[...].astype(f32)
        out_ref[4 + visit : 5 + visit, :] = jnp.sum(product, axis=0, keepdims=True)
    out_ref[7:8, :] = jnp.zeros((1, QW), f32)


def combine_stats(sc, visit, held):
    logs, deltas = [], []
    for j in range(VISITS):
        t = visit - j
        logs.append(jnp.where(sc[1] + t >= 0, held[t % NY][j : j + 1, :], masked))
        deltas.append(held[t % NY][4 + j : 5 + j, :])
    top = functools.reduce(jnp.maximum, logs)
    weights = [jnp.exp2(v - top) for v in logs]
    mass = sum(weights)
    weights = [v / mass for v in weights]
    return top + jnp.log2(mass), sum(a * b for a, b in zip(weights, deltas)), weights


def backward_kernel(lengths, *refs):
    sc = scalars(lengths)
    qs, dos, kvs, held, outs = refs[0:3], refs[3:6], refs[6:12], refs[12:16], refs[16:18]
    dq_ref, returns, own_ref, other_ref = refs[18], refs[19:21], refs[21], refs[22]
    keys, values, keys_t, q_all, do_all, dq_acc, logs, deltas, probs, dscores, dk, dv, q_t, do_t = refs[23:]
    load_keys(kvs, keys, values, keys_t, 0)
    dq_acc[...] = jnp.zeros_like(dq_acc)
    for visit in range(VISITS):
        q_all[visit] = qs[visit][...]
        do_all[visit] = dos[visit][...]
        turn_heads(qs[visit], q_t.at[visit])
        turn_heads(dos[visit], do_t.at[visit])
        log_total, delta, _ = combine_stats(sc, visit, held)
        logs[visit] = log_total
        deltas[visit] = delta

    @pl.loop(0, NZ // 2)
    def _(s):
        dk[...] = jnp.zeros_like(dk)
        dv[...] = jnp.zeros_like(dv)

        @pl.loop(0, VISITS)
        def _(visit):
            def work(allowed):
                for h in range(GROUP):
                    cols = slice(h * TOK, (h + 1) * TOK)
                    scores = dot(keys[s], q_t[visit, :, cols]) * (scale * log2e) - logs[visit, :, cols]
                    if allowed is not None:
                        scores = jnp.where(allowed, scores, masked)
                    p = jnp.exp2(scores)
                    dp = dot(values[s], do_t[visit, :, cols])
                    probs[:, cols] = p.astype(bf16)
                    dscores[:, cols] = (p * (dp - deltas[visit, :, cols])).astype(bf16)
                dv[...] += dot(probs[...], do_all[visit])
                dk[...] += dot(dscores[...], q_all[visit])
                dq_acc[visit] += dot(keys_t[s], dscores[...])

            on_tile(sc, visit, s, work)

        for e, out in enumerate((own_ref, other_ref)):
            for i in range(2):
                half = slice((i * NC + e) * TOK, (i * NC + e + 1) * TOK)
                out[2 * s + i, 0:TOK, :] = (dk[half, :] * scale).astype(bf16)
                out[2 * s + i, TOK:, :] = dv[half, :].astype(bf16)

    dq_ref[...] = dq_acc[0] * scale
    for visit in (1, 2):
        returns[visit - 1][0:HD, :] = outs[visit - 1][...]
        returns[visit - 1][HD:, :] = (dq_acc[visit] * scale).astype(bf16)


def context_kernel(lengths, o0, o1, o2, s0, s1, s2, s3, mh, _, send_ref, rows):
    sc = scalars(lengths)
    _, _, weights = combine_stats(sc, 0, (s0, s1, s2, s3))
    out = o0[...].astype(f32) * weights[0]
    for j, o in ((1, o1), (2, o2)):
        out = out + jnp.where(sc[1] >= j, o[0:HD, :].astype(f32), 0.0) * weights[j]
    for h in range(GROUP):
        rows[:, h * HD : (h + 1) * HD] = out[:, h * TOK : (h + 1) * TOK].T.astype(bf16)
    send_ref[...] = dot(mh[...], rows[...]).astype(bf16)


def add_cores_kernel(own, came, kept, below, above):
    for out, steps in ((kept, KEPT), (below, FROM_BELOW), (above, FROM_ABOVE)):
        for i, s in enumerate(steps):
            out[i] = (own[s].astype(f32) + came[s].astype(f32)).astype(out.dtype)


def add_near_kernel(kept, below, above, o0, o3, o5):
    o0[...] = kept[0] + below[0].astype(f32) + above[0].astype(f32)
    o3[...] = (kept[1] + below[1].astype(f32) + above[1].astype(f32)).astype(bf16)
    o5[...] = (kept[2] + below[2].astype(f32)).astype(bf16)


def rows_kernel(lengths, *refs):
    sc = scalars(lengths)
    parts, dqs, (cos, sin, rg_ref) = refs[0:3], refs[3:6], refs[6:9]
    c, s = cos[...], sin[...]
    dq = dqs[0][...]
    for j in (1, 2):
        dq = dq + jnp.where(sc[1] >= j, dqs[j][HD:, :].astype(f32), 0.0)
    for h in range(GROUP):
        rg_ref[:, h * HD : (h + 1) * HD] = turn_back(dq[:, h * TOK : (h + 1) * TOK].T, c, s).astype(bf16)
    dkv = sum(p[...].astype(f32) for p in parts)
    rg_ref[:, 512:640] = turn_back(dkv[0:TOK], c, s).astype(bf16)
    rg_ref[:, 640:768] = dkv[TOK:].astype(bf16)


def spread_kernel(lengths, *refs):
    sc = scalars(lengths)
    rg_ref, w, hids = refs[0], refs[1], refs[2:6]
    keep_ref, inner_ref, sends = refs[9], refs[10], refs[11:14]
    kept, sem = refs[14:]
    x = sc[4]
    rg = rg_ref[...]
    inner = jnp.zeros((TOK, 1), f32)
    for t in range(NX):
        first = pl.multiple_of((x + t) % NX * 512, 512)
        part = dot(rg, w[pl.ds(first, 512), :], NT)
        inner = inner + jnp.sum(part * hids[-t % NX][...].astype(f32), axis=1, keepdims=True)
        if t == 0:
            kept[...] = part
            keep_copy = pltpu.make_async_copy(kept, keep_ref, sem)
            keep_copy.start()
        else:
            sends[t - 1][0:TOK, :] = part.astype(bf16)
    row = jnp.broadcast_to(inner, (TOK, TOK)).T[0:16, :]
    inner_ref[...] = row[0:8, :]
    high = row.astype(bf16).astype(f32)
    line = lax.broadcasted_iota(i32, (16, TOK), 0)
    both = jnp.where(line == 0, high, jnp.where(line == 1, row - high, 0.0)).astype(bf16)
    for out in sends:
        out[TOK:, :] = jnp.concatenate([both, jnp.zeros((16, 384), bf16)], axis=1)
    keep_copy.wait()


def input_kernel(keep, inner, r1, r2, r3, inv_ref, hid, out_ref):
    total = keep[...]
    row = inner[0:1, :]
    for r in (r1, r2, r3):
        total = total + r[0:TOK, :].astype(f32)
        tail = r[TOK:, 0:TOK].astype(f32)
        row = row + tail[0:1, :] + tail[1:2, :]
    column = jnp.broadcast_to(row, (TOK, TOK)).T[:, 0:1]
    inv = inv_ref[:, 0:1]
    out_ref[...] = inv * total - hid[...].astype(f32) * (inv * inv * inv * column * (1.0 / (NX * 512)))


def weight_kernel(lengths, *refs):
    sc = scalars(lengths)
    ns, rgs, own_ref, other_ref = refs[0:4], refs[4:8], refs[8], refs[9]
    n_all, rg_all, product, sems = refs[10:]
    copies = [pltpu.make_async_copy(ns[t], n_all.at[pl.ds(t * TOK, TOK), :], sems.at[t]) for t in range(NY)]
    for copy in copies:
        copy.start()
    for t in range(NY):
        rg_all[t * TOK : (t + 1) * TOK, :] = rgs[t][...]
    for copy in copies:
        copy.wait()
    product[...] = dot(n_all[...], rg_all[...], TN)
    z, core = sc[2], sc[3]
    for s in range(NZ):
        first = ((z + NZ - s) % NZ) * 64
        own_ref[s] = product[pl.ds(pl.multiple_of(first + core * 32, 32), 32), :].astype(bf16)
        other_ref[s] = product[pl.ds(pl.multiple_of(first + (1 - core) * 32, 32), 32), :].astype(bf16)


def sum_kernel(*refs):
    refs[-1][...] = sum(r[...].astype(f32) for r in refs[:-1])


def index_of(y, z, c):
    return (y * NZ + z) * NC + c


def over_y(a, shift, wrap=True):
    pairs = [
        (index_of(y, z, c), index_of((y + shift) % NY, z, c))
        for y in range(NY)
        for z in range(NZ)
        for c in range(NC)
        if wrap or 0 <= y + shift < NY
    ]
    return lax.ppermute(a, "ctx", pairs)


def over_z(a, shift):
    pairs = [
        (index_of(y, z, c), index_of(y, (z + shift) % NZ, c))
        for y in range(NY)
        for z in range(NZ)
        for c in range(NC)
    ]
    return lax.ppermute(a, "ctx", pairs)


def over_c(a):
    pairs = [(index_of(y, z, c), index_of(y, z, 1 - c)) for y in range(NY) for z in range(NZ) for c in range(NC)]
    return lax.ppermute(a, "ctx", pairs)


def over_x(a, shift):
    return lax.ppermute(a, "fsdp", [(x, (x + shift) % NX) for x in range(NX)])


def exchange_slots(send):
    width = send.shape[1]
    groups = [[index_of(y, z, c) for y in range(NY) for z in range(NZ)] for c in range(NC)]
    came = lax.all_to_all(
        send.reshape(NY * NZ, NC * CAP, width), "ctx", split_axis=0, concat_axis=0, tiled=True, axis_index_groups=groups
    )
    return came.reshape(SLOTS, width)


def reduce_cores_and_z(own, other, name):
    shape = own.shape[1:]
    came = over_c(other)
    kept, below, above = call(
        add_cores_kernel,
        [((3,) + shape, f32), ((3,) + shape, bf16), ((2,) + shape, bf16)],
        "vv",
        (own, came),
        name="add_cores_" + name,
    )
    below, above = over_z(below, -1), over_z(above, 1)
    o0, o3, o5 = call(
        add_near_kernel,
        [(shape, f32), (shape, bf16), (shape, bf16)],
        "vvv",
        (kept, below, above),
        name="add_near_" + name,
    )
    return o0, over_z(o3, -3), over_z(o5, 3)


def shards(hidden, w, doc_lengths, owners, context_grad):
    lengths = doc_lengths.astype(i32)
    hids = [hidden] + [over_x(hidden, s) for s in range(1, NX)]

    grad_send, mh, from_owners, from_homes = call(
        route_kernel,
        [((SLOTS, QW), bf16), ((SLOTS, TOK), bf16), ((NC * SLOTS, TOK), bf16), ((NC * SLOTS, TOK), bf16)],
        "svv",
        (lengths, owners.reshape(N_CTX, TOK), context_grad),
        name="route",
    )
    arrived = exchange_slots(grad_send)

    home = lax.axis_index("ctx").astype(i32) * TOK + jnp.arange(TOK, dtype=i32)
    docs = jnp.arange(8, dtype=i32)
    doc_starts = jnp.sum(jnp.where(docs[:, None] > docs[None, :], lengths[None, :], 0), axis=1)
    start = jnp.max(jnp.where(home[:, None] >= doc_starts[None, :], doc_starts[None, :], 0), axis=1)
    frequency = rope_base ** (-(2.0 * jnp.arange(HD // 2, dtype=f32)) / HD)
    angles = (home - start).astype(f32)[:, None] * frequency[None, :]
    cos, sin = jnp.cos(angles), jnp.sin(angles)
    cos, sin = jnp.concatenate([cos, cos], axis=1), jnp.concatenate([-sin, sin], axis=1)

    q, kv, n0, n1, n2, n3, inv = call(
        project_kernel,
        [((QW, HD), bf16), ((2 * TOK, HD), bf16)] + [((TOK, 512), bf16)] * 4 + [((TOK, HD), f32)],
        "svvvvvvv",
        (lengths, *hids, w, cos, sin),
        scratch=[pltpu.VMEM((NX, TOK, 512), bf16), pltpu.SemaphoreType.DMA((NX,))],
        out_kinds="vvhhhhv",
        flops=4 * 10**8,
        moved=4 * 10**6,
        name="project",
    )
    qs = [q, over_y(q, -1, False), over_y(q, -2, False)]
    three, two = call(
        pack_kernel,
        [((3, 2 * TOK, HD), bf16), ((2, 2 * TOK, HD), bf16)],
        "vvvaa",
        (kv, over_z(kv, 3), over_z(kv, -3), qs[1], qs[2]),
        name="pack",
    )
    kv_own = [three, over_z(three, 1), over_z(two, -1)]
    kvs = kv_own + [over_c(a) for a in kv_own]
    ns = [n0] + [over_y(n, t) for t, n in ((1, n1), (2, n2), (3, n3))]

    (do,) = call(
        grad_home_kernel, [((QW, HD), bf16)], "vvv", (from_owners, arrived, over_c(arrived)), name="grad_home"
    )
    dos = [do, over_y(do, -1, False), over_y(do, -2, False)]

    *outs, stats = call(
        forward_kernel,
        [((HD, QW), bf16)] * 3 + [((8, QW), f32)],
        "s" + "v" * 9,
        (lengths, *qs, *kvs),
        scratch=[
            pltpu.VMEM((NZ // 2, TILE, HD), bf16),
            pltpu.VMEM((NZ // 2, TILE, HD), bf16),
            pltpu.VMEM((NZ // 2, HD, TILE), bf16),
            pltpu.VMEM((TILE, QW), bf16),
            pltpu.VMEM((HD, QW), f32),
            pltpu.VMEM((1, QW), f32),
            pltpu.VMEM((1, QW), f32),
            pltpu.VMEM((HD, QW), bf16),
        ],
        flops=3 * 10**9,
        name="forward",
    )
    (stats,) = call(delta_kernel, [((8, QW), f32)], "v" * 7, (stats, *outs, *dos), name="delta")
    held = [stats] + [over_y(stats, -t) for t in (1, 2, 3)]

    dq, back1, back2, dkv_own, dkv_other = call(
        backward_kernel,
        [((HD, QW), f32)] + [((2 * HD, QW), bf16)] * 2 + [((NZ, 2 * TOK, HD), bf16)] * 2,
        "s" + "v" * 18,
        (lengths, *qs, *dos, *kvs, *held, outs[1], outs[2]),
        scratch=[
            pltpu.VMEM((NZ // 2, TILE, HD), bf16),
            pltpu.VMEM((NZ // 2, TILE, HD), bf16),
            pltpu.VMEM((NZ // 2, HD, TILE), bf16),
            pltpu.VMEM((VISITS, QW, HD), bf16),
            pltpu.VMEM((VISITS, QW, HD), bf16),
            pltpu.VMEM((VISITS, HD, QW), f32),
            pltpu.VMEM((VISITS, 1, QW), f32),
            pltpu.VMEM((VISITS, 1, QW), f32),
            pltpu.VMEM((TILE, QW), bf16),
            pltpu.VMEM((TILE, QW), bf16),
            pltpu.VMEM((TILE, HD), f32),
            pltpu.VMEM((TILE, HD), f32),
            pltpu.VMEM((VISITS, HD, QW), bf16),
            pltpu.VMEM((VISITS, HD, QW), bf16),
        ],
        flops=5 * 10**9,
        name="backward",
    )
    back1, back2 = over_y(back1, 1, False), over_y(back2, 2, False)

    dkv_home = reduce_cores_and_z(dkv_own, dkv_other, "dkv")
    (rg,) = call(
        rows_kernel,
        [((TOK, 768), bf16)],
        "s" + "v" * 8,
        (lengths, *dkv_home, dq, back1, back2, cos, sin),
        name="rows",
    )
    rgs = [rg] + [over_y(rg, t) for t in (1, 2, 3)]
    keep, inner, *sends = call(
        spread_kernel,
        [((TOK, 512), f32), ((8, TOK), f32)] + [((TOK + 16, 512), bf16)] * 3,
        "svvvvvvaaa",
        (lengths, rg, w, *hids, *ns[1:]),
        scratch=[pltpu.VMEM((TOK, 512), f32), pltpu.SemaphoreType.DMA],
        name="spread",
        out_kinds="hvvvv",
    )
    (context_send,) = call(
        context_kernel,
        [((SLOTS, QW), bf16)],
        "s" + "v" * 8 + "a",
        (lengths, outs[0], back1, back2, *held, mh, inner),
        scratch=[pltpu.VMEM((TOK, QW), bf16)],
        name="context",
    )
    context_came = exchange_slots(context_send)

    totals = [over_x(a, t) for t, a in zip((1, 2, 3), sends)]
    w_own, w_other = call(
        weight_kernel,
        [((NZ, 32, 768), bf16)] * 2,
        "s" + "h" * 4 + "v" * 4,
        (lengths, *ns, *rgs),
        scratch=[
            pltpu.VMEM((NY * TOK, 512), bf16),
            pltpu.VMEM((NY * TOK, 768), bf16),
            pltpu.VMEM((512, 768), f32),
            pltpu.SemaphoreType.DMA((NY,)),
        ],
        flops=4 * 10**8,
        name="weight",
    )
    w_home = reduce_cores_and_z(w_own, w_other, "weight")
    (input_grad,) = call(
        input_kernel,
        [((TOK, 512), f32)],
        "v" * 7,
        (keep, inner, *totals, inv, hidden),
        name="input",
    )
    (context,) = call(
        place_kernel, [((TOK, QW), bf16)], "vvv", (from_homes, context_came, over_c(context_came)), name="place"
    )
    (weight_grad,) = call(sum_kernel, [((32, 768), f32)], "vvv", w_home, name="sum_weight")
    return context, input_grad, weight_grad


def solution(mesh):
    placed = (P("ctx", "fsdp"), P(None, "fsdp"), P(), P(), P("ctx", "fsdp"))
    return jax.shard_map(
        shards,
        mesh=mesh,
        in_specs=placed,
        out_specs=(P("ctx", "fsdp"), P("ctx", "fsdp"), P("ctx", "fsdp")),
        check_vma=False,
    )
```

```python
import functools

import jax
import jax.numpy as jnp
from jax import lax
from jax.experimental import pallas as pl
from jax.experimental.pallas import tpu as pltpu
from jax.sharding import PartitionSpec as P

HD = 128
GROUP = 4
TOK = 128
NY, NZ, NC = 4, 8, 2
N_CTX = NY * NZ * NC
NX = 4
CAP = 4
SLOTS = N_CTX * CAP
VISITS = 3
TILE = 512
KEPT = (0, 3, 5)
FROM_BELOW = (1, 4, 6)
FROM_ABOVE = (7, 2)
QW = GROUP * TOK
epsilon = 1e-05
rope_base = 500000.0
scale = HD ** (-0.5)
log2e = 1.4426950408889634
masked = -1e30

f32, bf16, i32 = jnp.float32, jnp.bfloat16, jnp.int32

NT = (((1,), (1,)), ((), ()))
NN = (((1,), (0,)), ((), ()))
TN = (((0,), (0,)), ((), ()))


def dot(a, b, dims=NN):
    return lax.dot_general(a, b, dims, preferred_element_type=f32)


def call(kernel, outs, in_kinds, args, scratch=(), flops=10**8, moved=2 * 10**6, name=None, out_kinds=None):
    vm = pl.BlockSpec(memory_space=pltpu.VMEM)
    sm = pl.BlockSpec(memory_space=pltpu.SMEM)
    hbm = pl.BlockSpec(memory_space=pltpu.HBM)
    anywhere = pl.BlockSpec(memory_space=pl.ANY)
    return pl.pallas_call(
        kernel,
        out_shape=[jax.ShapeDtypeStruct(s, d) for s, d in outs],
        in_specs=[{"s": sm, "v": vm, "h": hbm, "a": anywhere}[k] for k in in_kinds],
        out_specs=[{"v": vm, "h": hbm}[k] for k in out_kinds or "v" * len(outs)],
        scratch_shapes=list(scratch),
        compiler_params=pltpu.CompilerParams(vmem_limit_bytes=16 * 1024 * 1024),
        cost_estimate=pl.CostEstimate(flops=1000, bytes_accessed=1000, transcendentals=0),
        name=name,
    )(*args)


def scalars(lengths):
    me = lax.axis_index("ctx").astype(i32)
    x = lax.axis_index("fsdp").astype(i32)
    return [me, me // (NZ * NC), me // NC % NZ, me % NC, x, None, None, None] + [lengths[d] for d in range(8)]


def one_hot(condition):
    return jnp.where(condition, 1.0, 0.0).astype(bf16)


def route_kernel(lengths, owners, cg, send_ref, mh_ref, from_owners_ref, from_homes_ref):
    sc = scalars(lengths)
    me, core = sc[0], sc[3]
    mine = one_hot(owners[...] == me)
    count = dot(mine, jnp.ones((TOK, TOK), bf16)).astype(bf16)
    slot = lax.broadcasted_iota(i32, (SLOTS, TOK), 0)
    place = lax.broadcasted_iota(i32, (SLOTS, TOK), 1).astype(f32)
    rank = (slot % CAP).astype(f32)
    source = lax.broadcasted_iota(i32, (SLOTS, N_CTX), 1)
    slot_row = lax.broadcasted_iota(i32, (SLOTS, N_CTX), 0)

    def owned(home):
        base = dot(one_hot(source < home), count)
        here = dot(one_hot(source == home), count)
        return (base + rank == place) & (rank < here)

    send_ref[...] = dot(one_hot(owned(slot_row // CAP)), cg[...]).astype(bf16)
    for_me = slot // CAP % NC == core
    for e in range(NC):
        sender = slot_row // (NC * CAP) * NC + (core ^ e)
        from_homes_ref[e * SLOTS : (e + 1) * SLOTS, :] = one_hot(owned(sender) & for_me)

    own = jnp.broadcast_to(owners[pl.ds(me, 1), :].astype(f32), (TOK, TOK))
    earlier = lax.broadcasted_iota(i32, (TOK, TOK), 0) < lax.broadcasted_iota(i32, (TOK, TOK), 1)
    same = jnp.where((own == own.T) & earlier, 1.0, 0.0)
    own_rank = jnp.sum(same, axis=0, keepdims=True).astype(i32)
    owner = own[0:1, :].astype(i32)
    mh_ref[...] = one_hot(slot == owner * CAP + own_rank)
    came_slot = owner // NC * (NC * CAP) + core * CAP + own_rank
    for e in range(NC):
        here = (slot == came_slot) & (owner % NC == (core ^ e))
        from_owners_ref[e * SLOTS : (e + 1) * SLOTS, :] = one_hot(here)


def place_rows(matrix, same_core, other_core):
    rows = dot(matrix[0:SLOTS, :], same_core[...], TN) + dot(matrix[SLOTS:, :], other_core[...], TN)
    return rows.astype(bf16)


def grad_home_kernel(matrix, same_core, other_core, out_ref):
    rows = place_rows(matrix, same_core, other_core)
    for h in range(GROUP):
        out_ref[h * TOK : (h + 1) * TOK, :] = rows[:, h * HD : (h + 1) * HD]


def place_kernel(matrix, same_core, other_core, out_ref):
    out_ref[...] = place_rows(matrix, same_core, other_core)


def turn(t, c, s):
    return t * c + pltpu.roll(t, HD // 2, 1) * s


def turn_back(t, c, s):
    return t * c - pltpu.roll(t, HD // 2, 1) * s


def project_kernel(lengths, *refs):
    sc = scalars(lengths)
    hids, (w, cos, sin) = refs[0:4], refs[4:7]
    q_ref, kv_ref, *ns, inv_ref, held, out_sems = refs[7:]
    y, x = sc[1], sc[4]
    blocks = [h[...].astype(f32) for h in hids]
    square = sum(jnp.sum(b * b, axis=1, keepdims=True) for b in blocks)
    inv = lax.rsqrt(square * (1.0 / (NX * 512)) + epsilon)
    inv_ref[...] = jnp.broadcast_to(inv, (TOK, HD))
    for s in range(NX):
        held[(x + NX - s) % NX] = (blocks[s] * inv).astype(bf16)
    out_copies = [
        pltpu.make_async_copy(held.at[(y + t) % NX], out, out_sems.at[t]) for t, out in enumerate(ns)
    ]
    for copy in out_copies:
        copy.start()
    total = jnp.zeros((TOK, 768), f32)
    for k in range(NX):
        total = total + dot(held[k], w[k * 512 : (k + 1) * 512, :])
    c, s = cos[...], sin[...]
    for h in range(GROUP):
        q_ref[h * TOK : (h + 1) * TOK, :] = turn(total[:, h * HD : (h + 1) * HD], c, s).astype(bf16)
    kv_ref[0:TOK, :] = turn(total[:, 512:640], c, s).astype(bf16)
    kv_ref[TOK:, :] = total[:, 640:768].astype(bf16)
    for copy in out_copies:
        copy.wait()


def turn_heads(rows, out):
    for h in range(GROUP):
        part = slice(h * TOK, (h + 1) * TOK)
        out[:, part] = rows[part, :].astype(f32).T.astype(bf16)


def doc_start(sc, row):
    start, begin = 0, sc[8]
    for d in range(1, 8):
        start = jnp.where(begin <= row, begin, start)
        begin = begin + sc[8 + d]
    return start


def first_query(sc, visit):
    return ((sc[1] + visit) * NZ * NC + sc[2] * NC + sc[3]) * TOK


def key_tile(sc, s):
    return sc[1] * NZ + (sc[2] + NZ - s) % NZ


def tile_state(sc, visit, s):
    first, low = first_query(sc, visit), key_tile(sc, s) * (NC * TOK)
    high = low + NC * TOK - 1
    some = (sc[1] + visit < NY) & (low <= first + TOK - 1) & (high >= doc_start(sc, first))
    every = (high <= first) & (low >= doc_start(sc, first + TOK - 1))
    return some, every


def tile_mask(sc, visit, s):
    rows = first_query(sc, visit) + lax.broadcasted_iota(i32, (1, TOK), 1)
    starts = doc_start(sc, rows)
    line = lax.broadcasted_iota(i32, (TILE, TOK), 0)
    offset = (line % (NC * TOK)) ^ (sc[3] * TOK)
    first, second = key_tile(sc, 2 * s) * (NC * TOK), key_tile(sc, 2 * s + 1) * (NC * TOK)
    key_rows = jnp.where(line < NC * TOK, first, second) + offset
    return (key_rows >= starts) & (key_rows <= rows)


def on_tile(sc, visit, s, work):
    some, every = tile_state(sc, visit, 2 * s)
    some2, every2 = tile_state(sc, visit, 2 * s + 1)
    some, every = some | some2, every & every2

    @pl.when(some & every)
    def _():
        work(None)

    @pl.when(some & jnp.logical_not(every))
    def _():
        work(tile_mask(sc, visit, s))


def load_keys(kvs, keys, values, turned, which):
    for e in range(NC):
        for stack, steps in zip(kvs[3 * e : 3 * e + 3], (KEPT, FROM_BELOW, FROM_ABOVE)):
            for i, s in enumerate(steps):
                at = s // 2
                half = slice((s % 2 * NC + e) * TOK, (s % 2 * NC + e + 1) * TOK)
                keys[at, half, :] = stack[i, 0:TOK, :]
                values[at, half, :] = stack[i, TOK:, :]
                picked = stack[i, which * TOK : (which + 1) * TOK, :]
                turned[at, :, half] = picked.astype(f32).T.astype(bf16)


def pack_kernel(b0, b3, b5, _, __, three_ref, two_ref):
    for i, b in enumerate((b0, b3, b5)):
        three_ref[i] = b[...]
        if i < 2:
            two_ref[i] = b[...]


def forward_kernel(lengths, *refs):
    sc = scalars(lengths)
    qs, kvs = refs[0:3], refs[3:9]
    outs, stats = refs[9:12], refs[12]
    keys, values, values_t, probs, acc, top, total, q_t = refs[13:]
    load_keys(kvs, keys, values, values_t, 1)
    stats[...] = jnp.zeros_like(stats)
    for visit in range(VISITS):
        turn_heads(qs[visit], q_t)
        acc[...] = jnp.zeros_like(acc)
        total[...] = jnp.zeros_like(total)
        top[...] = jnp.full_like(top, masked)

        @pl.loop(0, NZ // 2)
        def _(s):
            def work(allowed):
                for h in range(GROUP):
                    cols = slice(h * TOK, (h + 1) * TOK)
                    scores = dot(keys[s], q_t[:, cols])
                    if allowed is not None:
                        scores = jnp.where(allowed, scores, masked)
                    old = top[:, cols]
                    new = jnp.maximum(old, jnp.max(scores, axis=0, keepdims=True))
                    base = jnp.maximum(new, 0.1 * masked) * (scale * log2e)
                    p = jnp.exp2(scores * (scale * log2e) - base)
                    fade = jnp.exp2(old * (scale * log2e) - base)
                    top[:, cols] = new
                    total[:, cols] = total[:, cols] * fade + jnp.sum(p, axis=0, keepdims=True)
                    probs[:, cols] = p.astype(bf16)
                    acc[:, cols] = acc[:, cols] * fade
                acc[...] += dot(values_t[s], probs[...])

            on_tile(sc, visit, s, work)

        mass = total[...]
        some = mass > 0.0
        mass = jnp.where(some, mass, 1.0)
        outs[visit][...] = (acc[...] * (1.0 / mass)).astype(bf16)
        logs = top[...] * (scale * log2e) + jnp.log2(mass)
        stats[visit : visit + 1, :] = jnp.where(some, logs, masked)


def delta_kernel(stats, o0, o1, o2, d0, d1, d2, out_ref):
    out_ref[0:4, :] = stats[0:4, :]
    for visit, (o, d) in enumerate(((o0, d0), (o1, d1), (o2, d2))):
        product = d[...].astype(f32).T * o[...].astype(f32)
        out_ref[4 + visit : 5 + visit, :] = jnp.sum(product, axis=0, keepdims=True)
    out_ref[7:8, :] = jnp.zeros((1, QW), f32)


def combine_stats(sc, visit, held):
    logs, deltas = [], []
    for j in range(VISITS):
        t = visit - j
        logs.append(jnp.where(sc[1] + t >= 0, held[t % NY][j : j + 1, :], masked))
        deltas.append(held[t % NY][4 + j : 5 + j, :])
    top = functools.reduce(jnp.maximum, logs)
    weights = [jnp.exp2(v - top) for v in logs]
    mass = sum(weights)
    weights = [v / mass for v in weights]
    return top + jnp.log2(mass), sum(a * b for a, b in zip(weights, deltas)), weights


def backward_kernel(lengths, *refs):
    sc = scalars(lengths)
    qs, dos, kvs, held, outs = refs[0:3], refs[3:6], refs[6:12], refs[12:16], refs[16:18]
    dq_ref, returns, own_ref, other_ref = refs[18], refs[19:21], refs[21], refs[22]
    keys, values, keys_t, q_all, do_all, dq_acc, logs, deltas, probs, dscores, dk, dv, q_t, do_t = refs[23:]
    load_keys(kvs, keys, values, keys_t, 0)
    dq_acc[...] = jnp.zeros_like(dq_acc)
    for visit in range(VISITS):
        q_all[visit] = qs[visit][...]
        do_all[visit] = dos[visit][...]
        turn_heads(qs[visit], q_t.at[visit])
        turn_heads(dos[visit], do_t.at[visit])
        log_total, delta, _ = combine_stats(sc, visit, held)
        logs[visit] = log_total
        deltas[visit] = delta

    @pl.loop(0, NZ // 2)
    def _(s):
        dk[...] = jnp.zeros_like(dk)
        dv[...] = jnp.zeros_like(dv)

        @pl.loop(0, VISITS)
        def _(visit):
            def work(allowed):
                for h in range(GROUP):
                    cols = slice(h * TOK, (h + 1) * TOK)
                    scores = dot(keys[s], q_t[visit, :, cols]) * (scale * log2e) - logs[visit, :, cols]
                    if allowed is not None:
                        scores = jnp.where(allowed, scores, masked)
                    p = jnp.exp2(scores)
                    dp = dot(values[s], do_t[visit, :, cols])
                    probs[:, cols] = p.astype(bf16)
                    dscores[:, cols] = (p * (dp - deltas[visit, :, cols])).astype(bf16)
                dv[...] += dot(probs[...], do_all[visit])
                dk[...] += dot(dscores[...], q_all[visit])
                dq_acc[visit] += dot(keys_t[s], dscores[...])

            on_tile(sc, visit, s, work)

        for e, out in enumerate((own_ref, other_ref)):
            for i in range(2):
                half = slice((i * NC + e) * TOK, (i * NC + e + 1) * TOK)
                out[2 * s + i, 0:TOK, :] = (dk[half, :] * scale).astype(bf16)
                out[2 * s + i, TOK:, :] = dv[half, :].astype(bf16)

    dq_ref[...] = dq_acc[0] * scale
    for visit in (1, 2):
        returns[visit - 1][0:HD, :] = outs[visit - 1][...]
        returns[visit - 1][HD:, :] = (dq_acc[visit] * scale).astype(bf16)


def context_kernel(lengths, o0, o1, o2, s0, s1, s2, s3, mh, _, send_ref, rows):
    sc = scalars(lengths)
    _, _, weights = combine_stats(sc, 0, (s0, s1, s2, s3))
    out = o0[...].astype(f32) * weights[0]
    for j, o in ((1, o1), (2, o2)):
        out = out + jnp.where(sc[1] >= j, o[0:HD, :].astype(f32), 0.0) * weights[j]
    for h in range(GROUP):
        rows[:, h * HD : (h + 1) * HD] = out[:, h * TOK : (h + 1) * TOK].T.astype(bf16)
    send_ref[...] = dot(mh[...], rows[...]).astype(bf16)


def add_cores_kernel(own, came, kept, below, above):
    for out, steps in ((kept, KEPT), (below, FROM_BELOW), (above, FROM_ABOVE)):
        for i, s in enumerate(steps):
            out[i] = (own[s].astype(f32) + came[s].astype(f32)).astype(out.dtype)


def add_near_kernel(kept, below, above, o0, o3, o5):
    o0[...] = kept[0] + below[0].astype(f32) + above[0].astype(f32)
    o3[...] = (kept[1] + below[1].astype(f32) + above[1].astype(f32)).astype(bf16)
    o5[...] = (kept[2] + below[2].astype(f32)).astype(bf16)


def rows_kernel(lengths, *refs):
    sc = scalars(lengths)
    parts, dqs, (cos, sin, rg_ref) = refs[0:3], refs[3:6], refs[6:9]
    c, s = cos[...], sin[...]
    dq = dqs[0][...]
    for j in (1, 2):
        dq = dq + jnp.where(sc[1] >= j, dqs[j][HD:, :].astype(f32), 0.0)
    for h in range(GROUP):
        rg_ref[:, h * HD : (h + 1) * HD] = turn_back(dq[:, h * TOK : (h + 1) * TOK].T, c, s).astype(bf16)
    dkv = sum(p[...].astype(f32) for p in parts)
    rg_ref[:, 512:640] = turn_back(dkv[0:TOK], c, s).astype(bf16)
    rg_ref[:, 640:768] = dkv[TOK:].astype(bf16)


def spread_kernel(lengths, *refs):
    sc = scalars(lengths)
    rg_ref, w, hids = refs[0], refs[1], refs[2:6]
    keep_ref, inner_ref, sends = refs[9], refs[10], refs[11:14]
    kept, sem = refs[14:]
    x = sc[4]
    rg = rg_ref[...]
    inner = jnp.zeros((TOK, 1), f32)
    for t in range(NX):
        first = pl.multiple_of((x + t) % NX * 512, 512)
        part = dot(rg, w[pl.ds(first, 512), :], NT)
        inner = inner + jnp.sum(part * hids[-t % NX][...].astype(f32), axis=1, keepdims=True)
        if t == 0:
            kept[...] = part
            keep_copy = pltpu.make_async_copy(kept, keep_ref, sem)
            keep_copy.start()
        else:
            sends[t - 1][0:TOK, :] = part.astype(bf16)
    row = jnp.broadcast_to(inner, (TOK, TOK)).T[0:16, :]
    inner_ref[...] = row[0:8, :]
    high = row.astype(bf16).astype(f32)
    line = lax.broadcasted_iota(i32, (16, TOK), 0)
    both = jnp.where(line == 0, high, jnp.where(line == 1, row - high, 0.0)).astype(bf16)
    for out in sends:
        out[TOK:, :] = jnp.concatenate([both, jnp.zeros((16, 384), bf16)], axis=1)
    keep_copy.wait()


def input_kernel(keep, inner, r1, r2, r3, inv_ref, hid, out_ref):
    total = keep[...]
    row = inner[0:1, :]
    for r in (r1, r2, r3):
        total = total + r[0:TOK, :].astype(f32)
        tail = r[TOK:, 0:TOK].astype(f32)
        row = row + tail[0:1, :] + tail[1:2, :]
    column = jnp.broadcast_to(row, (TOK, TOK)).T[:, 0:1]
    inv = inv_ref[:, 0:1]
    out_ref[...] = inv * total - hid[...].astype(f32) * (inv * inv * inv * column * (1.0 / (NX * 512)))


def weight_kernel(lengths, *refs):
    sc = scalars(lengths)
    ns, rgs, own_ref, other_ref = refs[0:4], refs[4:8], refs[8], refs[9]
    n_all, rg_all, product, sems = refs[10:]
    copies = [pltpu.make_async_copy(ns[t], n_all.at[pl.ds(t * TOK, TOK), :], sems.at[t]) for t in range(NY)]
    for copy in copies:
        copy.start()
    for t in range(NY):
        rg_all[t * TOK : (t + 1) * TOK, :] = rgs[t][...]
    for copy in copies:
        copy.wait()
    product[...] = dot(n_all[...], rg_all[...], TN)
    z, core = sc[2], sc[3]
    for s in range(NZ):
        first = ((z + NZ - s) % NZ) * 64
        own_ref[s] = product[pl.ds(pl.multiple_of(first + core * 32, 32), 32), :].astype(bf16)
        other_ref[s] = product[pl.ds(pl.multiple_of(first + (1 - core) * 32, 32), 32), :].astype(bf16)


def sum_kernel(*refs):
    refs[-1][...] = sum(r[...].astype(f32) for r in refs[:-1])


def index_of(y, z, c):
    return (y * NZ + z) * NC + c


def over_y(a, shift):
    pairs = [
        (index_of(y, z, c), index_of((y + shift) % NY, z, c))
        for y in range(NY)
        for z in range(NZ)
        for c in range(NC)
    ]
    return lax.ppermute(a, "ctx", pairs)


def over_z(a, shift):
    pairs = [
        (index_of(y, z, c), index_of(y, (z + shift) % NZ, c))
        for y in range(NY)
        for z in range(NZ)
        for c in range(NC)
    ]
    return lax.ppermute(a, "ctx", pairs)


def over_c(a):
    pairs = [(index_of(y, z, c), index_of(y, z, 1 - c)) for y in range(NY) for z in range(NZ) for c in range(NC)]
    return lax.ppermute(a, "ctx", pairs)


def over_x(a, shift):
    return lax.ppermute(a, "fsdp", [(x, (x + shift) % NX) for x in range(NX)])


def exchange_slots(send):
    width = send.shape[1]
    groups = [[index_of(y, z, c) for y in range(NY) for z in range(NZ)] for c in range(NC)]
    came = lax.all_to_all(
        send.reshape(NY * NZ, NC * CAP, width), "ctx", split_axis=0, concat_axis=0, tiled=True, axis_index_groups=groups
    )
    return came.reshape(SLOTS, width)


def reduce_cores_and_z(own, other, name):
    shape = own.shape[1:]
    came = over_c(other)
    kept, below, above = call(
        add_cores_kernel,
        [((3,) + shape, f32), ((3,) + shape, bf16), ((2,) + shape, bf16)],
        "vv",
        (own, came),
        name="add_cores_" + name,
    )
    below, above = over_z(below, -1), over_z(above, 1)
    o0, o3, o5 = call(
        add_near_kernel,
        [(shape, f32), (shape, bf16), (shape, bf16)],
        "vvv",
        (kept, below, above),
        name="add_near_" + name,
    )
    return o0, over_z(o3, -3), over_z(o5, 3)


def shards(hidden, w, doc_lengths, owners, context_grad):
    lengths = doc_lengths.astype(i32)
    hids = [hidden] + [over_x(hidden, s) for s in range(1, NX)]

    grad_send, mh, from_owners, from_homes = call(
        route_kernel,
        [((SLOTS, QW), bf16), ((SLOTS, TOK), bf16), ((NC * SLOTS, TOK), bf16), ((NC * SLOTS, TOK), bf16)],
        "svv",
        (lengths, owners.reshape(N_CTX, TOK), context_grad),
        name="route",
    )
    arrived = exchange_slots(grad_send)

    home = lax.axis_index("ctx").astype(i32) * TOK + jnp.arange(TOK, dtype=i32)
    docs = jnp.arange(8, dtype=i32)
    doc_starts = jnp.sum(jnp.where(docs[:, None] > docs[None, :], lengths[None, :], 0), axis=1)
    start = jnp.max(jnp.where(home[:, None] >= doc_starts[None, :], doc_starts[None, :], 0), axis=1)
    frequency = rope_base ** (-(2.0 * jnp.arange(HD // 2, dtype=f32)) / HD)
    angles = (home - start).astype(f32)[:, None] * frequency[None, :]
    cos, sin = jnp.cos(angles), jnp.sin(angles)
    cos, sin = jnp.concatenate([cos, cos], axis=1), jnp.concatenate([-sin, sin], axis=1)

    q, kv, n0, n1, n2, n3, inv = call(
        project_kernel,
        [((QW, HD), bf16), ((2 * TOK, HD), bf16)] + [((TOK, 512), bf16)] * 4 + [((TOK, HD), f32)],
        "svvvvvvv",
        (lengths, *hids, w, cos, sin),
        scratch=[pltpu.VMEM((NX, TOK, 512), bf16), pltpu.SemaphoreType.DMA((NX,))],
        out_kinds="vvhhhhv",
        flops=4 * 10**8,
        moved=4 * 10**6,
        name="project",
    )
    qs = [q, over_y(q, -1), over_y(q, -2)]
    three, two = call(
        pack_kernel,
        [((3, 2 * TOK, HD), bf16), ((2, 2 * TOK, HD), bf16)],
        "vvvaa",
        (kv, over_z(kv, 3), over_z(kv, -3), qs[1], qs[2]),
        name="pack",
    )
    kv_own = [three, over_z(three, 1), over_z(two, -1)]
    kvs = kv_own + [over_c(a) for a in kv_own]
    ns = [n0] + [over_y(n, t) for t, n in ((1, n1), (2, n2), (3, n3))]

    (do,) = call(
        grad_home_kernel, [((QW, HD), bf16)], "vvv", (from_owners, arrived, over_c(arrived)), name="grad_home"
    )
    dos = [do, over_y(do, -1), over_y(do, -2)]

    *outs, stats = call(
        forward_kernel,
        [((HD, QW), bf16)] * 3 + [((8, QW), f32)],
        "s" + "v" * 9,
        (lengths, *qs, *kvs),
        scratch=[
            pltpu.VMEM((NZ // 2, TILE, HD), bf16),
            pltpu.VMEM((NZ // 2, TILE, HD), bf16),
            pltpu.VMEM((NZ // 2, HD, TILE), bf16),
            pltpu.VMEM((TILE, QW), bf16),
            pltpu.VMEM((HD, QW), f32),
            pltpu.VMEM((1, QW), f32),
            pltpu.VMEM((1, QW), f32),
            pltpu.VMEM((HD, QW), bf16),
        ],
        flops=3 * 10**9,
        name="forward",
    )
    (stats,) = call(delta_kernel, [((8, QW), f32)], "v" * 7, (stats, *outs, *dos), name="delta")
    held = [stats] + [over_y(stats, -t) for t in (1, 2, 3)]

    dq, back1, back2, dkv_own, dkv_other = call(
        backward_kernel,
        [((HD, QW), f32)] + [((2 * HD, QW), bf16)] * 2 + [((NZ, 2 * TOK, HD), bf16)] * 2,
        "s" + "v" * 18,
        (lengths, *qs, *dos, *kvs, *held, outs[1], outs[2]),
        scratch=[
            pltpu.VMEM((NZ // 2, TILE, HD), bf16),
            pltpu.VMEM((NZ // 2, TILE, HD), bf16),
            pltpu.VMEM((NZ // 2, HD, TILE), bf16),
            pltpu.VMEM((VISITS, QW, HD), bf16),
            pltpu.VMEM((VISITS, QW, HD), bf16),
            pltpu.VMEM((VISITS, HD, QW), f32),
            pltpu.VMEM((VISITS, 1, QW), f32),
            pltpu.VMEM((VISITS, 1, QW), f32),
            pltpu.VMEM((TILE, QW), bf16),
            pltpu.VMEM((TILE, QW), bf16),
            pltpu.VMEM((TILE, HD), f32),
            pltpu.VMEM((TILE, HD), f32),
            pltpu.VMEM((VISITS, HD, QW), bf16),
            pltpu.VMEM((VISITS, HD, QW), bf16),
        ],
        flops=5 * 10**9,
        name="backward",
    )
    back1, back2 = over_y(back1, 1), over_y(back2, 2)

    dkv_home = reduce_cores_and_z(dkv_own, dkv_other, "dkv")
    (rg,) = call(
        rows_kernel,
        [((TOK, 768), bf16)],
        "s" + "v" * 8,
        (lengths, *dkv_home, dq, back1, back2, cos, sin),
        name="rows",
    )
    rgs = [rg] + [over_y(rg, t) for t in (1, 2, 3)]
    keep, inner, *sends = call(
        spread_kernel,
        [((TOK, 512), f32), ((8, TOK), f32)] + [((TOK + 16, 512), bf16)] * 3,
        "svvvvvvaaa",
        (lengths, rg, w, *hids, *ns[1:]),
        scratch=[pltpu.VMEM((TOK, 512), f32), pltpu.SemaphoreType.DMA],
        name="spread",
        out_kinds="hvvvv",
    )
    (context_send,) = call(
        context_kernel,
        [((SLOTS, QW), bf16)],
        "s" + "v" * 8 + "a",
        (lengths, outs[0], back1, back2, *held, mh, inner),
        scratch=[pltpu.VMEM((TOK, QW), bf16)],
        name="context",
    )
    context_came = exchange_slots(context_send)

    totals = [over_x(a, t) for t, a in zip((1, 2, 3), sends)]
    w_own, w_other = call(
        weight_kernel,
        [((NZ, 32, 768), bf16)] * 2,
        "s" + "h" * 4 + "v" * 4,
        (lengths, *ns, *rgs),
        scratch=[
            pltpu.VMEM((NY * TOK, 512), bf16),
            pltpu.VMEM((NY * TOK, 768), bf16),
            pltpu.VMEM((512, 768), f32),
            pltpu.SemaphoreType.DMA((NY,)),
        ],
        flops=4 * 10**8,
        name="weight",
    )
    w_home = reduce_cores_and_z(w_own, w_other, "weight")
    (input_grad,) = call(
        input_kernel,
        [((TOK, 512), f32)],
        "v" * 7,
        (keep, inner, *totals, inv, hidden),
        name="input",
    )
    (context,) = call(
        place_kernel, [((TOK, QW), bf16)], "vvv", (from_homes, context_came, over_c(context_came)), name="place"
    )
    (weight_grad,) = call(sum_kernel, [((32, 768), f32)], "vvv", w_home, name="sum_weight")
    return context, input_grad, weight_grad


def solution(mesh):
    placed = (P("ctx", "fsdp"), P(None, "fsdp"), P(), P(), P("ctx", "fsdp"))
    return jax.shard_map(
        shards,
        mesh=mesh,
        in_specs=placed,
        out_specs=(P("ctx", "fsdp"), P("ctx", "fsdp"), P("ctx", "fsdp")),
        check_vma=False,
    )
```
